128 devices in a mesh: blk: 16 (over z, x_lo, core), uly: 8 (over x_hi, y).
Axes of the slice: x: 4 (x_hi: 2, x_lo: 2; x = x_hi * 2 + x_lo), y: 4, z: 4, core: 2. Of those that a mesh axis runs over, the one named last changes fastest.
Arguments:
- queries: bfloat16 [18432, 5120], P(('blk', 'uly')), may hold values from -6 to 6
- keys: bfloat16 [36864, 5120], P(('blk', 'uly')), may hold values from -6 to 6
- values: bfloat16 [36864, 5120], P(('blk', 'uly')), may hold values from -6 to 6
- tile_lists: int32 [48, 12], replicated, may hold values from 0 to 95, as said below
- tile_counts: int32 [48], replicated, may hold values from 3 to 12, as said below
Outputs:
- attended: bfloat16 [18432, 5120], P(('blk', 'uly'))
The draws below stay inside these ranges and needn't reach their ends.
Inputs may be any that keep to these rules, and one draw needn't show every extreme that they name: `tile_lists`: entries lie in tiles of the latent frames from two before to two after the query tile's frame (frames are 3 tiles, blocks two frames); entry 0 is the query tile itself; the first tile_counts entries are distinct; the others repeat entry 0. `tile_counts`: counts vary from tile to tile; at least 3.
All inputs are finite; a program needn't handle non-finite values.
Results may differ from the reference program's by a relative error of at most 0.017.
Values may be sent and summed in bfloat16 or wider, within the bound.
A program may use at most 192 MiB of HBM per device.

```python
import jax
import jax.numpy as jnp
from jax import lax

HEADS = 40
HD = 128
TILE = 384
FT = 3
MAXT = 12
D = 5120
TOKENS = 36864
TILES = 96
QTILES = 48
QTOK = 18432


def tile_plan(key):
    key = jax.random.fold_in(key, 7)
    key_pick, key_count = jax.random.split(key)
    query_ids = jnp.arange(QTILES, dtype=jnp.int32)
    shard_ids = query_ids // FT
    within = query_ids % FT
    offsets = jnp.arange(5 * FT, dtype=jnp.int32)
    candidate = (2 * shard_ids[:, None] - 2) * FT + offsets[None, :]
    usable = (candidate >= 0) & (candidate < TILES)
    own_tile = 2 * shard_ids * FT + within
    raw_score = jax.random.randint(key_pick, (QTILES, 5 * FT), 0, 1 << 20)
    score_table = jnp.where(candidate == own_tile[:, None], 1 << 29, jnp.where(usable, raw_score * 256 + offsets[None, :], -1 - offsets[None, :]))
    top_scores, picked = lax.top_k(score_table, MAXT)
    chosen = jnp.take_along_axis(candidate, picked, axis=1)
    upper_count = jnp.minimum(jnp.sum(usable.astype(jnp.int32), axis=1), MAXT)
    counts_drawn = 3 + jax.random.randint(key_count, (QTILES,), 0, 1 << 20) % (upper_count - 2)
    counts_drawn = counts_drawn.at[FT].set(MAXT).at[0].set(3)
    slot_ids = jnp.arange(MAXT, dtype=jnp.int32)
    lists_out = jnp.where(slot_ids[None, :] < counts_drawn[:, None], chosen, own_tile[:, None])
    return (lists_out.astype(jnp.int32), counts_drawn.astype(jnp.int32))


def draw_tile_lists(key, part):
    lists_out, counts_drawn = tile_plan(key)
    return lists_out


def draw_tile_counts(key, part):
    lists_out, counts_drawn = tile_plan(key)
    return counts_drawn


def draw_queries(key, part):
    key = jax.random.fold_in(key, 21)
    return jnp.clip(jax.random.normal(key, (QTOK, D), jnp.float32), -6.0, 6.0).astype(jnp.bfloat16)


def draw_keys(key, part):
    key = jax.random.fold_in(key, 33)
    return jnp.clip(jax.random.normal(key, (TOKENS, D), jnp.float32), -6.0, 6.0).astype(jnp.bfloat16)


def levels(stream_key, shape, cuts, low, top_value):
    def one(dim, blocks):
        heights = jax.random.uniform(jax.random.fold_in(jax.random.fold_in(stream_key, 6), dim), (blocks,), jnp.float32, low / len(cuts), top_value / len(cuts))
        return jnp.repeat(jnp.exp(heights), shape[dim] // blocks).reshape((-1,) + (1,) * (len(shape) - dim - 1))

    level = one(*cuts[0])
    for cut in cuts[1:]:
        level = level * one(*cut)
    return level


def bell_draw(own_key, extent, spread, limit, shards=(), held_as=jnp.bfloat16):
    values = spread * jax.random.normal(own_key, extent, jnp.float32)
    if shards:
        values = values * levels(own_key, extent, shards, -0.22, 0.18)
    return jnp.clip(values, -limit, limit).astype(held_as)


def setup_inputs(seed: int = 0) -> dict:
    key_of = jax.random.split(jax.random.key(seed), 6)
    return {
        "queries": draw_queries(jax.random.fold_in(key_of[5], 71), 0),
        "keys": draw_keys(jax.random.fold_in(key_of[5], 71), 0),
        "values": bell_draw(key_of[2], (TOKENS, D), 1.0, 6.0, ((0, 128),)),
        "tile_lists": draw_tile_lists(jax.random.fold_in(key_of[5], 71), 0),
        "tile_counts": draw_tile_counts(jax.random.fold_in(key_of[5], 71), 0),
    }


def attend_tile(query_tile, key_rows, value_rows, usable):
    score_scale = HD ** -0.5
    scores = jnp.einsum("qhd,khd->hqk", query_tile.astype(jnp.float32), key_rows.astype(jnp.float32)) * score_scale
    scores = jnp.where(usable[None, None, :], scores, -1e30)
    peak = jnp.max(scores, axis=-1, keepdims=True)
    weights = jnp.where(usable[None, None, :], jnp.exp(scores - peak), 0.0)
    denominator = jnp.sum(weights, axis=-1)
    rounded = lax.optimization_barrier(weights.astype(jnp.bfloat16)).astype(jnp.float32)
    summed = jnp.einsum("hqk,khd->qhd", rounded, value_rows.astype(jnp.float32))
    return (summed / jnp.transpose(denominator)[:, :, None]).astype(jnp.bfloat16)


def reference(queries, keys, values, tile_lists, tile_counts):
    query_tiles = queries.reshape(QTILES, TILE, HEADS, HD)
    key_tiles = keys.reshape(TILES, TILE, HEADS, HD)
    value_tiles = values.reshape(TILES, TILE, HEADS, HD)
    slot_ids = jnp.arange(MAXT, dtype=jnp.int32)

    def one_tile(inputs):
        query_tile, listed, count_here = inputs
        key_rows = jnp.take(key_tiles, listed, axis=0).reshape(MAXT * TILE, HEADS, HD)
        value_rows = jnp.take(value_tiles, listed, axis=0).reshape(MAXT * TILE, HEADS, HD)
        usable = jnp.repeat(slot_ids < count_here, TILE)
        return attend_tile(query_tile, key_rows, value_rows, usable)

    attended = lax.map(one_tile, (query_tiles, tile_lists, tile_counts))
    return attended.reshape(QTOK, D)
```

```python
import functools

import jax
import jax.numpy as jnp
from jax import lax
from jax.experimental import pallas as pl
from jax.experimental.pallas import tpu as pltpu
from jax.sharding import PartitionSpec as P

HD = 128
TILE = 384
FT = 3
MAXT = 12
HEADS = 40
BLOCK = 2304
HALF = 1152
KROWS = 288
QROWS = 144
MAIN = 32
LEFT = 5 * BLOCK + HALF
KV_ROWS = LEFT + 3 * BLOCK + HALF
UNITS = 6
MESH = pl.DeviceIdType.MESH
OFFSETS = [(dx, (k - dx) % 4) for k in (1, 3, 2, 0) for dx in (1, 3, 2, 0)]


class Place:
    def __init__(self):
        blk, uly = lax.axis_index("blk"), lax.axis_index("uly")
        self.z, self.b, self.u = blk // 4, blk % 4, uly
        self.c = blk % 2
        self.xl = self.b // 2
        self.x = (uly // 4) * 2 + self.xl
        self.y = uly % 4
        self.chip = self.x * 4 + self.y
        self.odd = (self.x + self.y) % 2
        self.heavy = self.odd == 0

    def at(self, z, x, y, c):
        return (z * 4 + (x % 2) * 2 + c, (x // 2) * 4 + y)


def greet(me):
    barrier = pltpu.get_barrier_semaphore()

    def hello(z, x, y, c):
        pl.semaphore_signal(barrier, inc=1, device_id=me.at(z, x, y, c), device_id_type=MESH)

    for dx, dy in OFFSETS:
        x, y = (me.x + dx) % 4, (me.y + dy) % 4
        if (dx, dy) != (0, 0):
            hello(me.z, x, y, me.c)
        hello(me.z, x, y, 1 - me.c)
    return barrier, hello


def exchange_kernel(q, k, v, qo, ko, vo, send, left_send, main_in, left_in, q_in, fwd_send, fwd_in):
    me = Place()
    barrier, hello = greet(me)

    @pl.when(me.z > 0)
    def _():
        hello(me.z - 1, me.x, me.y, 0)
        hello(me.z - 1, me.x, me.y, 1)

    @pl.when(me.z < 3)
    def _():
        hello(me.z + 1, me.x, me.y, 0)
        hello(me.z + 1, me.x, me.y, 1)

    above = jnp.where(me.z < 3, 2, 0)
    below = jnp.where(me.z > 0, 2, 0)
    pl.semaphore_wait(barrier, 31 + above + below)

    def columns(head):
        return pl.ds(pl.multiple_of(head * HD, HD), HD)

    def rows(start, size):
        return pl.ds(pl.multiple_of(start, 16), size)

    def scatter(source, target, size, main_row, left_row, s, main_sem, left_sem):
        for dx, dy in OFFSETS:
            x, y = (me.x + dx) % 4, (me.y + dy) % 4
            for dc in (0, 1):
                c = me.c if dc == 0 else 1 - me.c
                src = source.at[:, columns((x * 4 + y) * 2 + c)]
                dst = target.at[rows(main_row, size), :]
                if (dx, dy, dc) == (0, 0, 0):
                    pltpu.make_async_copy(src, dst, main_sem).start()
                else:
                    pltpu.make_async_remote_copy(
                        src, dst, send.at[s], main_sem, device_id=me.at(me.z, x, y, c), device_id_type=MESH
                    ).start()
        for k2 in (2, 0):
            for dx in (1, 3, 2, 0):
                x = (me.x + dx) % 4
                y = (me.y + me.odd + k2 + 4 - dx) % 4
                src = source.at[:, columns(MAIN + (x * 4 + y) // 2)]
                dst = target.at[rows(left_row, size), :]

                def away():
                    pltpu.make_async_remote_copy(
                        src, dst, left_send.at[s], left_sem, device_id=me.at(me.z, x, y, me.xl), device_id_type=MESH
                    ).start()

                if (k2, dx) != (0, 0):
                    away()
                else:
                    own = jnp.logical_and(me.heavy, me.xl == me.c)

                    @pl.when(own)
                    def _():
                        pltpu.make_async_copy(src, dst, left_sem).start()

                    @pl.when(jnp.logical_not(own))
                    def _():
                        away()

    e = me.b % 2
    kv_main = BLOCK * (1 + me.b) + me.u * KROWS
    kv_left = LEFT + BLOCK * (1 + e) + me.u * KROWS

    def arrived(target, start, size, sem):
        ref = target.at[pl.ds(start, size), :]
        pltpu.make_async_copy(ref, ref, sem).wait()

    def forward(i, target, src, dst, size, device):
        return pltpu.make_async_remote_copy(
            target.at[pl.ds(src, size), :], target.at[pl.ds(dst, size), :],
            fwd_send.at[i], fwd_in.at[i], device_id=device, device_id_type=MESH,
        )

    not_last, not_first = me.z < 3, me.z > 0
    heavy = me.heavy
    up_left = jnp.logical_and(heavy, jnp.logical_or(me.c == 0, not_last))
    down_left = jnp.logical_and(heavy, jnp.logical_or(me.c == 1, not_first))
    from_prev = jnp.logical_and(heavy, jnp.logical_or(me.c == 1, not_first))
    from_next = jnp.logical_and(heavy, jnp.logical_or(me.c == 0, not_last))

    def copies(a, target):
        return (
            forward(4 * a, target, BLOCK * 4, 0, BLOCK, me.at(me.z + 1, me.x, me.y, me.c)),
            forward(4 * a + 1, target, BLOCK, 5 * BLOCK, HALF, me.at(me.z - 1, me.x, me.y, me.c)),
            forward(4 * a + 2, target, LEFT + 2 * BLOCK, LEFT, BLOCK, me.at(me.z + me.c, me.x, me.y, 1 - me.c)),
            forward(4 * a + 3, target, LEFT + BLOCK, LEFT + 3 * BLOCK, HALF,
                    me.at(me.z - 1 + me.c, me.x, me.y, 1 - me.c)),
        )

    def pass_on(a, target):
        up, down, left_up, left_down = copies(a, target)
        arrived(target, BLOCK * 4, BLOCK, main_in.at[4 * a + 3])

        @pl.when(not_last)
        def _():
            up.start()

        arrived(target, BLOCK, BLOCK, main_in.at[4 * a])

        @pl.when(not_first)
        def _():
            down.start()

        @pl.when(heavy)
        def _():
            arrived(target, LEFT + 2 * BLOCK, BLOCK, left_in.at[2 * a + 1])

            @pl.when(up_left)
            def _():
                left_up.start()

            arrived(target, LEFT + BLOCK, BLOCK, left_in.at[2 * a])

            @pl.when(down_left)
            def _():
                left_down.start()

    scatter(k, ko, KROWS, kv_main, kv_left, 0, main_in.at[me.b], left_in.at[e])
    scatter(v, vo, KROWS, kv_main, kv_left, 1, main_in.at[4 + me.b], left_in.at[2 + e])
    pass_on(0, ko)
    scatter(q, qo, QROWS, HALF * me.b + me.u * QROWS, HALF * (4 + e) + me.u * QROWS, 2, q_in.at[0], q_in.at[1])
    pass_on(1, vo)

    for a, target in ((0, ko), (1, vo)):
        arrived(target, BLOCK * 2, BLOCK, main_in.at[4 * a + 1])
        arrived(target, BLOCK * 3, BLOCK, main_in.at[4 * a + 2])
    arrived(qo, 0, 4 * HALF, q_in.at[0])

    @pl.when(heavy)
    def _():
        arrived(qo, 4 * HALF, 2 * HALF, q_in.at[1])

    for a, target in ((0, ko), (1, vo)):
        up, down, left_up, left_down = copies(a, target)
        for copy, sent, got in (
            (up, not_last, not_first),
            (down, not_first, not_last),
            (left_up, up_left, from_prev),
            (left_down, down_left, from_next),
        ):
            @pl.when(sent)
            def _():
                copy.wait_send()

            @pl.when(got)
            def _():
                copy.wait_recv()

    own = jnp.logical_and(heavy, me.xl == me.c)
    for s, source in enumerate((k, v, q)):
        def sent(n, sem):
            ref = source.at[:, pl.ds(0, n * HD)]
            pltpu.make_async_copy(ref, ref, sem).wait()

        sent(31, send.at[s])

        @pl.when(own)
        def _():
            sent(7, left_send.at[s])

        @pl.when(jnp.logical_not(own))
        def _():
            sent(8, left_send.at[s])


def exchange(q, k, v):
    anywhere = pl.BlockSpec(memory_space=pl.ANY)
    dma = pltpu.SemaphoreType.DMA
    return pl.pallas_call(
        exchange_kernel,
        out_shape=(
            jax.ShapeDtypeStruct((UNITS * HALF, HD), jnp.bfloat16),
            jax.ShapeDtypeStruct((KV_ROWS, HD), jnp.bfloat16),
            jax.ShapeDtypeStruct((KV_ROWS, HD), jnp.bfloat16),
        ),
        in_specs=[anywhere] * 3,
        out_specs=(anywhere,) * 3,
        scratch_shapes=[dma((3,)), dma((3,)), dma((8,)), dma((4,)), dma((2,)), dma((8,)), dma((8,))],
        compiler_params=pltpu.CompilerParams(collective_id=0, has_side_effects=True),
        name="exchange",
    )(q, k, v)


def attend_kernel(lists, counts, place, q, k, v, out):
    unit, t = pl.program_id(0), pl.program_id(1)
    z, c, heavy = place[0], place[1], place[2]
    shared = unit >= 4
    block = 4 * z + jnp.where(shared, 2 * c + unit - 4, unit)
    tile = block * FT + t
    first = jnp.where(shared, 33 - (4 * z + 2 * c - 1) * 6, -(4 * z - 1) * 6)
    scale = HD ** (-0.5) * 1.4426950408889634

    @pl.when(jnp.logical_or(unit < 4, heavy > 0))
    def _():
        query = q[...]
        ones = jnp.ones((TILE, HD), jnp.bfloat16)

        def scores(m):
            row = pl.multiple_of((lists[tile, m] + first) * TILE, TILE)
            s = lax.dot_general(
                query, k[pl.ds(row, TILE), :], (((1,), (1,)), ((), ())), preferred_element_type=jnp.float32
            )
            return s, row

        def weighted(s, peak, row):
            w = jnp.exp2((s - peak) * scale).astype(jnp.bfloat16)
            both = jnp.concatenate([v[pl.ds(row, TILE), :], ones], axis=1)
            return jnp.dot(w, both, preferred_element_type=jnp.float32)

        s, row = scores(0)
        peak = jnp.max(s, axis=1, keepdims=True)
        total = weighted(s, peak, row)

        def step(m, carry):
            peak, total = carry
            s, row = scores(m)
            higher = jnp.maximum(peak, jnp.max(s, axis=1, keepdims=True))
            return higher, total * jnp.exp2((peak - higher) * scale) + weighted(s, higher, row)

        peak, total = lax.fori_loop(1, counts[tile], step, (peak, total))
        out[...] = (total[:, :HD] / total[:, HD:]).astype(jnp.bfloat16)


def attend(lists, counts, place, q, k, v):
    whole = pl.BlockSpec((KV_ROWS, HD), lambda unit, t, *_: (0, 0))
    tile = pl.BlockSpec((TILE, HD), lambda unit, t, *_: (unit * FT + t, 0))
    return pl.pallas_call(
        attend_kernel,
        out_shape=jax.ShapeDtypeStruct((UNITS * HALF, HD), jnp.bfloat16),
        grid_spec=pltpu.PrefetchScalarGridSpec(
            num_scalar_prefetch=3,
            grid=(UNITS, FT),
            in_specs=[tile, whole, whole],
            out_specs=tile,
        ),
        compiler_params=pltpu.CompilerParams(vmem_limit_bytes=48 * 1024 * 1024),
        name="attend",
    )(lists, counts, place, q, k, v)


def collect_kernel(a, out, send, left_send, arrive):
    me = Place()
    barrier, _ = greet(me)
    pl.semaphore_wait(barrier, 31)

    def one(row, head, x, y, c, local, sem):
        src = a.at[pl.ds(pl.multiple_of(row, 16), QROWS), :]
        dst = out.at[:, pl.ds(pl.multiple_of(head * HD, HD), HD)]
        if local:
            pltpu.make_async_copy(src, dst, arrive).start()
        else:
            pltpu.make_async_remote_copy(
                src, dst, sem, arrive, device_id=me.at(me.z, x, y, c), device_id_type=MESH
            ).start()

    for dx, dy in OFFSETS:
        x, y = (me.x + dx) % 4, (me.y + dy) % 4
        b, u = x % 2, (x // 2) * 4 + y
        for dc in (0, 1):
            c = me.c if dc == 0 else 1 - me.c
            one((2 * b + c) * HALF + u * QROWS, me.chip * 2 + me.c, x, y, c, (dx, dy, dc) == (0, 0, 0), send)

    @pl.when(me.heavy)
    def _():
        for dh, dy in ((0, 1), (1, 3), (1, 2), (0, 3), (1, 1), (0, 2), (1, 0), (0, 0)):
            x = (me.x // 2 * 2 + 2 * dh + me.c) % 4
            y = (me.y + dy) % 4
            u = (x // 2) * 4 + y
            for dc in (0, 1):
                c = me.c if dc == 0 else 1 - me.c
                row, head = (4 + c) * HALF + u * QROWS, MAIN + me.chip // 2
                if (dh, dy, dc) != (0, 0, 0):
                    one(row, head, x, y, c, False, left_send)
                else:
                    @pl.when(me.xl == me.c)
                    def _():
                        one(row, head, x, y, c, True, left_send)

                    @pl.when(me.xl != me.c)
                    def _():
                        one(row, head, x, y, c, False, left_send)

    pltpu.make_async_copy(out, out, arrive).wait()

    def sent(n, sem):
        ref = a.at[pl.ds(0, n * QROWS), :]
        pltpu.make_async_copy(ref, ref, sem).wait()

    sent(31, send)

    @pl.when(jnp.logical_and(me.heavy, me.xl == me.c))
    def _():
        sent(15, left_send)

    @pl.when(jnp.logical_and(me.heavy, me.xl != me.c))
    def _():
        sent(16, left_send)


def collect(a):
    dma = pltpu.SemaphoreType.DMA
    return pl.pallas_call(
        collect_kernel,
        out_shape=jax.ShapeDtypeStruct((QROWS, HEADS * HD), jnp.bfloat16),
        in_specs=[pl.BlockSpec(memory_space=pl.ANY)],
        out_specs=pl.BlockSpec(memory_space=pl.ANY),
        scratch_shapes=[dma, dma, dma],
        compiler_params=pltpu.CompilerParams(collective_id=1, has_side_effects=True),
        name="collect",
    )(a)


def per_device(queries, keys, values, tile_lists, tile_counts):
    me = Place()
    place = jnp.stack([me.z, me.c, 1 - me.odd]).astype(jnp.int32)
    q, k, v = exchange(queries, keys, values)
    return collect(attend(tile_lists, tile_counts, place, q, k, v))


def solution(mesh):
    placed = (P(("blk", "uly"), None), P(("blk", "uly"), None), P(("blk", "uly"), None), P(), P())
    return jax.shard_map(
        per_device, mesh=mesh, in_specs=placed, out_specs=P(("blk", "uly"), None), check_vma=False
    )
```

```python
import functools

import jax
import jax.numpy as jnp
from jax import lax
from jax.experimental import pallas as pl
from jax.experimental.pallas import tpu as pltpu
from jax.sharding import PartitionSpec as P

HD = 128
TILE = 384
FT = 3
MAXT = 12
HEADS = 40
BLOCK = 2304
HALF = 1152
KROWS = 288
QROWS = 144
MAIN = 32
PAIR = 3 * BLOCK + HALF
ONE = 2 * BLOCK + HALF
VROWS = HD + 16
G = 2
GROUPS = MAXT // G
LOG2_SCALE = HD ** (-0.5) * 1.4426950408889634
FAR = 1e30
MESH = pl.DeviceIdType.MESH
OFFSETS = [(dx, (k - dx) % 4) for k in (1, 3, 2, 0) for dx in (1, 3, 2, 0)]
PAIR_OFFSETS = ((1, 0), (2, 1), (3, 0), (0, 1), (1, 1), (2, 0), (3, 1), (0, 0))
HALF_OFFSETS = ((0, 1), (1, 3), (1, 2), (0, 3), (1, 1), (0, 2), (1, 0), (0, 0))


def rows(start, size):
    return pl.ds(pl.multiple_of(start, 16), size)


def columns(head):
    return pl.ds(pl.multiple_of(head * HD, HD), HD)


def arrived(ref, sem):
    pltpu.make_async_copy(ref, ref, sem).wait()


def kernel(
    lists, counts, q, k, v, out,
    qa, qb, ql, ka, kb, kl, va, vb, vl, done, kt, vt, qt, s0, s1, acc,
    send, got, q_got, fwd_send, fwd_got, halo_send, halo_got, out_send, out_got,
):
    blk, u = lax.axis_index("blk"), lax.axis_index("uly")
    z, b, c = blk // 4, blk % 4, blk % 2
    xl = b // 2
    x, y = (u // 4) * 2 + xl, u % 4
    chip = x * 4 + y
    quarter = (y % 2) * 2 + c
    not_first, not_last = z > 0, z < 3
    mine = xl == c
    mine_l = xl == y % 2
    no = jnp.logical_not
    both = jnp.logical_and
    either = jnp.logical_or

    def at(z, x, y, c):
        return (z * 4 + (x % 2) * 2 + c, (x // 2) * 4 + y)

    def remote(src, dst, send_sem, recv_sem, device):
        return pltpu.make_async_remote_copy(
            src, dst, send_sem, recv_sem, device_id=device, device_id_type=MESH
        )

    barrier = pltpu.get_barrier_semaphore()

    def hello(device):
        pl.semaphore_signal(barrier, inc=1, device_id=device, device_id_type=MESH)

    for dx, dy in OFFSETS:
        there = ((x + dx) % 4, (y + dy) % 4)
        if (dx, dy) != (0, 0):
            hello(at(z, *there, c))
        hello(at(z, *there, 1 - c))
    up = either(c == 0, not_last)
    down = either(c == 1, not_first)

    @pl.when(both(c == 0, not_first))
    def _():
        hello(at(z - 1, x, y, 1))

    @pl.when(both(c == 1, not_last))
    def _():
        hello(at(z + 1, x, y, 0))

    @pl.when(both(quarter == 0, not_first))
    def _():
        for i in range(8):
            hello(at(z - 1, (i // 4) * 2 + 1, i % 4, 1))

    @pl.when(both(quarter == 3, not_last))
    def _():
        for i in range(4):
            hello(at(z + 1, 0, i, 0))

    halo_up = both(b == 3, not_last)
    halo_down = both(both(b == 0, u < 4), not_first)
    pl.semaphore_wait(
        barrier,
        31
        + jnp.where(both(c == 1, not_last), 1, 0)
        + jnp.where(both(c == 0, not_first), 1, 0)
        + jnp.where(halo_up, 8, 0)
        + jnp.where(halo_down, 8, 0),
    )

    e = b % 2

    def scatter(r, source, target, row, size, s, sem):
        for dx, dy in OFFSETS:
            px, py = (x + dx) % 4, (y + dy) % 4
            src = source.at[:, columns((px * 4 + py) * 2 + r)]
            dst = target.at[rows(row, size), :]

            def away():
                remote(src, dst, send.at[s], sem, at(z, px, py, xl)).start()

            if (dx, dy) != (0, 0):
                away()
            else:
                @pl.when(mine)
                def _():
                    pltpu.make_async_copy(src, dst, sem).start()

                @pl.when(no(mine))
                def _():
                    away()

    def scatter_shared(source, target, row, size, s, sem):
        for dx, dp in PAIR_OFFSETS:
            px, pp = (x + dx) % 4, (y // 2 + dp) % 2
            src = source.at[:, columns(MAIN + px * 2 + pp)]
            dst = target.at[rows(row, size), :]

            def away():
                remote(src, dst, send.at[s], sem, at(z, px, pp * 2 + xl, e)).start()

            if (dx, dp) != (0, 0):
                away()
            else:
                @pl.when(mine_l)
                def _():
                    pltpu.make_async_copy(src, dst, sem).start()

                @pl.when(no(mine_l))
                def _():
                    away()

    sends_prev = either(b == 1, halo_up)
    sends_next = either(both(b == 2, u < 4), halo_down)

    def scatter_halo(source, target, a):
        @pl.when(sends_prev)
        def _():
            up_z, odd = jnp.where(b == 3, 1, 0), jnp.where(b == 1, 1, 0)
            for dx, dp in PAIR_OFFSETS:
                px, pp = (x + dx) % 4, (y // 2 + dp) % 2
                remote(
                    source.at[:, columns(MAIN + px * 2 + pp)], target.at[rows(u * KROWS, KROWS), :],
                    halo_send.at[a], halo_got.at[a], at(z + up_z, px, pp * 2 + odd, 0),
                ).start()

        @pl.when(sends_next)
        def _():
            down_z = jnp.where(b == 0, 1, 0)
            for dx, dp in PAIR_OFFSETS:
                px, pp = (x + dx) % 4, (y // 2 + dp) % 2
                remote(
                    source.at[:, columns(MAIN + px * 2 + pp)],
                    target.at[rows(2 * BLOCK + (u % 4) * KROWS, KROWS), :],
                    halo_send.at[a], halo_got.at[a], at(z - down_z, px, pp * 2 + down_z, 1),
                ).start()

    kv_row, q_row = BLOCK * (1 + e) + u * KROWS, HALF * e + u * QROWS

    def send_k(r, target):
        scatter(r, k, target, kv_row, KROWS, 3 * r, got.at[4 * r + e])

    def send_v(r, target):
        scatter(r, v, target, kv_row, KROWS, 3 * r + 1, got.at[4 * r + 2 + e])

    def send_q(r, target):
        scatter(r, q, target, q_row, QROWS, 3 * r + 2, q_got.at[r])

    def halos(i, target):
        return (
            remote(
                target.at[pl.ds(2 * BLOCK, BLOCK), :], target.at[pl.ds(0, BLOCK), :],
                fwd_send.at[2 * i], fwd_got.at[2 * i], at(z + c, x, y, 1 - c),
            ),
            remote(
                target.at[pl.ds(BLOCK, HALF), :], target.at[pl.ds(3 * BLOCK, HALF), :],
                fwd_send.at[2 * i + 1], fwd_got.at[2 * i + 1], at(z - 1 + c, x, y, 1 - c),
            ),
        )

    from_prev, from_next = either(c == 1, not_first), either(c == 0, not_last)

    def pass_on(i, target):
        to_up, to_down = halos(i, target)
        arrived(target.at[pl.ds(2 * BLOCK, BLOCK), :], got.at[2 * i + 1])

        @pl.when(up)
        def _():
            to_up.start()

        arrived(target.at[pl.ds(BLOCK, BLOCK), :], got.at[2 * i])

        @pl.when(down)
        def _():
            to_down.start()

    def halos_in(i, target):
        to_up, to_down = halos(i, target)

        @pl.when(from_prev)
        def _():
            to_up.wait_recv()

        @pl.when(from_next)
        def _():
            to_down.wait_recv()

    def halos_sent(i, target):
        to_up, to_down = halos(i, target)

        @pl.when(up)
        def _():
            to_up.wait_send()

        @pl.when(down)
        def _():
            to_down.wait_send()

    def shared_halo(a, target):
        return (
            remote(
                target.at[pl.ds(BLOCK, BLOCK), :], target.at[pl.ds(0, BLOCK), :],
                fwd_send.at[8 + a], fwd_got.at[8 + a], at(z, x, y, 1),
            ),
            remote(
                target.at[pl.ds(BLOCK, HALF), :], target.at[pl.ds(2 * BLOCK, HALF), :],
                fwd_send.at[8 + a], fwd_got.at[8 + a], at(z, x, y, 0),
            ),
        )

    def shared_pass_on(a, target):
        to_other, to_first = shared_halo(a, target)
        arrived(target.at[pl.ds(BLOCK, BLOCK), :], got.at[8 + a])

        @pl.when(c == 0)
        def _():
            to_other.start()

        @pl.when(c == 1)
        def _():
            to_first.start()

    def shared_in(a, target):
        to_other, to_first = shared_halo(a, target)

        @pl.when(both(c == 0, either(quarter == 2, not_first)))
        def _():
            arrived(target.at[pl.ds(0, BLOCK), :], halo_got.at[a])

        @pl.when(both(c == 1, either(quarter == 1, not_last)))
        def _():
            arrived(target.at[pl.ds(2 * BLOCK, HALF), :], halo_got.at[a])

        @pl.when(c == 0)
        def _():
            to_other.wait_send()
            to_first.wait_recv()

        @pl.when(c == 1)
        def _():
            to_first.wait_send()
            to_other.wait_recv()

    def lay_out(keys, values, tiles):
        def one(t, carry):
            row = pl.ds(pl.multiple_of(t * TILE, TILE), TILE)
            kt[t] = keys[row, :]
            vt[t, 0:HD, :] = values[row, :].T
            return carry

        lax.fori_loop(0, tiles, one, 0)

    def attend(queries, query_row, block, first_block, done_row, tiles):
        def scale(t, carry):
            row = pl.multiple_of(query_row + t * TILE, TILE)
            query = queries[pl.ds(row, TILE), :].astype(jnp.float32).T * LOG2_SCALE
            high = query.astype(jnp.bfloat16)
            qt[t, 0:HD, :] = high
            qt[t, HD:2 * HD, :] = (query - high.astype(jnp.float32)).astype(jnp.bfloat16)
            return carry

        lax.fori_loop(0, FT, scale, 0)
        first = first_block * 6

        def place(tile, m):
            return jnp.clip(lists[tile, m] - first, 0, tiles - 1)

        def scores(buffer, t, g):
            tile = block * FT + t
            top = None
            for j in range(G):
                key = kt[place(tile, g * G + j)]
                s = jnp.dot(jnp.concatenate([key, key], axis=1), qt[t], preferred_element_type=jnp.float32)
                buffer[j * TILE:(j + 1) * TILE, :] = s
                t_top = jnp.max(s, axis=0, keepdims=True)
                top = t_top if top is None else jnp.maximum(top, t_top)
            return top

        def weigh(buffer, t, g, peak):
            tile = block * FT + t
            total = None
            for j in range(G):
                m = g * G + j
                shift = peak + jnp.maximum(m + 1 - counts[tile], 0).astype(jnp.float32) * FAR
                w = jnp.exp2(buffer[j * TILE:(j + 1) * TILE, :] - shift).astype(jnp.bfloat16)
                part = jnp.dot(vt[place(tile, m)], w, preferred_element_type=jnp.float32)
                total = part if total is None else total + part
            return total

        def query_tile(t, peak):
            acc[...] = jnp.zeros_like(acc)

            def step(i, peak):
                g = 2 * i
                top = scores(s1, t, g + 1)
                part = weigh(s0, t, g, peak)
                higher = jnp.maximum(peak, top)
                acc[...] = (acc[...] + part) * jnp.exp2(peak - higher)
                after = jnp.where(g + 2 < GROUPS, 0, 1)
                top = scores(s0, jnp.minimum(t + after, FT - 1), (g + 2) * (1 - after))
                part = weigh(s1, t, g + 1, higher)
                highest = jnp.where(after == 1, top, jnp.maximum(higher, top))
                acc[...] = (acc[...] + part) * jnp.where(after == 1, 1.0, jnp.exp2(higher - highest))
                return highest

            peak = lax.fori_loop(0, GROUPS // 2, step, peak)
            total = acc[...]
            row = pl.multiple_of(done_row + t * TILE, TILE)
            done[pl.ds(row, TILE), :] = (total[:HD] / total[HD:HD + 1]).T.astype(jnp.bfloat16)
            return peak

        lax.fori_loop(0, FT, query_tile, scores(s0, 0, 0))

    def give_back(done_row, head, half, core, local, s):
        for dh, dy in HALF_OFFSETS:
            px, py = (x // 2 * 2 + 2 * dh + half) % 4, (y + dy) % 4
            src = done.at[rows(done_row + ((px // 2) * 4 + py) * QROWS, QROWS), :]
            dst = out.at[:, columns(head)]

            def away():
                remote(src, dst, out_send.at[s], out_got, at(z, px, py, core)).start()

            if (dh, dy) != (0, 0):
                away()
            else:
                @pl.when(local)
                def _():
                    pltpu.make_async_copy(src, dst, out_got).start()

                @pl.when(no(local))
                def _():
                    away()

    def unit(queries, r, e):
        attend(queries, e * HALF, 4 * z + 2 * c + e, 4 * z + 2 * c - 1, (2 * r + e) * HALF, PAIR // TILE)
        give_back((2 * r + e) * HALF, chip * 2 + r, c, e, both(mine, c == e), r)

    send_k(0, ka)
    send_v(0, va)
    send_q(0, qa)
    vt[:, HD:VROWS, :] = jnp.ones((vt.shape[0], VROWS - HD, TILE), jnp.bfloat16)
    pass_on(0, ka)
    send_k(1, kb)
    pass_on(1, va)
    send_v(1, vb)
    send_q(1, qb)
    arrived(qa, q_got.at[0])
    halos_in(0, ka)
    halos_in(1, va)
    lay_out(ka, va, PAIR // TILE)
    unit(qa, 0, 0)
    pass_on(2, kb)
    scatter_shared(k, kl, BLOCK + u * KROWS, KROWS, 6, got.at[8])
    scatter_halo(k, kl, 0)
    unit(qa, 0, 1)
    pass_on(3, vb)
    scatter_shared(v, vl, BLOCK + u * KROWS, KROWS, 7, got.at[9])
    scatter_halo(v, vl, 1)
    scatter_shared(q, ql, u * QROWS, QROWS, 8, q_got.at[2])
    arrived(qb, q_got.at[1])
    halos_in(2, kb)
    halos_in(3, vb)
    lay_out(kb, vb, PAIR // TILE)
    unit(qb, 1, 0)
    shared_pass_on(0, kl)
    unit(qb, 1, 1)
    shared_pass_on(1, vl)
    arrived(ql, q_got.at[2])
    shared_in(0, kl)
    shared_in(1, vl)
    lay_out(kl, vl, ONE // TILE)
    attend(ql, 0, 4 * z + quarter, 4 * z + quarter - 1, 4 * HALF, ONE // TILE)
    give_back(4 * HALF, MAIN + chip // 2, y % 2, c, mine_l, 2)

    for i, target in enumerate((ka, va, kb, vb)):
        halos_sent(i, target)

    def sent(source, many, fewer, n, sem):
        for condition, size in ((fewer, n - 1), (no(fewer), n)):
            @pl.when(condition)
            def _():
                arrived(many(source, size), sem)

    def heads(source, n):
        return source.at[:, pl.ds(0, n * HD)]

    def parts(source, n):
        return source.at[pl.ds(0, n * QROWS), :]

    for a, source in enumerate((k, v, q)):
        sent(source, heads, mine, 16, send.at[a])
        sent(source, heads, mine, 16, send.at[3 + a])
        sent(source, heads, mine_l, 8, send.at[6 + a])
    for a, source in enumerate((k, v)):
        @pl.when(either(sends_prev, sends_next))
        def _():
            arrived(heads(source, 8), halo_send.at[a])
    sent(done, parts, mine, 16, out_send.at[0])
    sent(done, parts, mine, 16, out_send.at[1])
    sent(done, parts, mine_l, 8, out_send.at[2])
    arrived(out, out_got)


def per_device(queries, keys, values, tile_lists, tile_counts):
    anywhere = pl.BlockSpec(memory_space=pl.ANY)
    scalars = pl.BlockSpec(memory_space=pltpu.SMEM)
    dma = pltpu.SemaphoreType.DMA

    def held(n):
        return pltpu.VMEM((n, HD), jnp.bfloat16)

    return pl.pallas_call(
        kernel,
        out_shape=jax.ShapeDtypeStruct((QROWS, HEADS * HD), jnp.bfloat16),
        in_specs=[scalars, scalars, anywhere, anywhere, anywhere],
        out_specs=anywhere,
        scratch_shapes=[
            held(2 * HALF), held(2 * HALF), held(HALF),
            held(PAIR), held(PAIR), held(ONE),
            held(PAIR), held(PAIR), held(ONE),
            held(5 * HALF),
            pltpu.VMEM((PAIR // TILE, TILE, HD), jnp.bfloat16),
            pltpu.VMEM((PAIR // TILE, VROWS, TILE), jnp.bfloat16),
            pltpu.VMEM((FT, 2 * HD, TILE), jnp.bfloat16),
            pltpu.VMEM((G * TILE, TILE), jnp.float32),
            pltpu.VMEM((G * TILE, TILE), jnp.float32),
            pltpu.VMEM((VROWS, TILE), jnp.float32),
            dma((9,)), dma((10,)), dma((3,)), dma((10,)), dma((10,)), dma((2,)), dma((2,)), dma((3,)), dma,
        ],
        compiler_params=pltpu.CompilerParams(
            collective_id=0, has_side_effects=True, vmem_limit_bytes=60 * 1024 * 1024
        ),
        name="attention",
    )(tile_lists, tile_counts, queries, keys, values)


def solution(mesh):
    placed = (P(("blk", "uly"), None), P(("blk", "uly"), None), P(("blk", "uly"), None), P(), P())
    return jax.shard_map(
        per_device, mesh=mesh, in_specs=placed, out_specs=P(("blk", "uly"), None), check_vma=False
    )
```

```python
import functools

import jax
import jax.numpy as jnp
from jax import lax
from jax.experimental import pallas as pl
from jax.experimental.pallas import tpu as pltpu
from jax.sharding import PartitionSpec as P

HD = 128
TILE = 384
FT = 3
MAXT = 12
HEADS = 40
BLOCK = 2304
HALF = 1152
KROWS = 288
QROWS = 144
MAIN = 32
PAIR = 3 * BLOCK + HALF
ONE = 2 * BLOCK + HALF
VROWS = HD + 16
G = 3
GROUPS = MAXT // G
LOG2_SCALE = HD ** (-0.5) * 1.4426950408889634
FAR = 1e30
MESH = pl.DeviceIdType.MESH
OFFSETS = [(dx, (k - dx) % 4) for k in (1, 3, 2, 0) for dx in (1, 3, 2, 0)]
PAIR_OFFSETS = ((1, 0), (2, 1), (3, 0), (0, 1), (1, 1), (2, 0), (3, 1), (0, 0))
HALF_OFFSETS = ((0, 1), (1, 3), (1, 2), (0, 3), (1, 1), (0, 2), (1, 0), (0, 0))


def rows(start, size):
    return pl.ds(pl.multiple_of(start, 16), size)


def columns(head):
    return pl.ds(pl.multiple_of(head * HD, HD), HD)


def arrived(ref, sem):
    pltpu.make_async_copy(ref, ref, sem).wait()


def kernel(
    lists_in, counts_in, q, k, v, out,
    lists, counts, list_sem, qa, qb, ql, ka, kb, kl, va, vb, vl, done, kt, vt, qt, s0, s1, acc, kept, peaks,
    send, got, q_got, fwd_send, fwd_got, halo_send, halo_got, out_send, out_got,
):
    blk, u = lax.axis_index("blk"), lax.axis_index("uly")
    z, b, c = blk // 4, blk % 4, blk % 2
    xl = b // 2
    x, y = (u // 4) * 2 + xl, u % 4
    chip = x * 4 + y
    side = (y + z) % 2
    quarter = side * 2 + c
    outer = jnp.logical_or(quarter == 0, quarter == 3)
    not_first, not_last = z > 0, z < 3
    mine = xl == c
    mine_l = xl == side
    no = jnp.logical_not
    both = jnp.logical_and
    either = jnp.logical_or

    def at(z, x, y, c):
        return (z * 4 + (x % 2) * 2 + c, (x // 2) * 4 + y)

    def remote(src, dst, send_sem, recv_sem, device):
        return pltpu.make_async_remote_copy(
            src, dst, send_sem, recv_sem, device_id=device, device_id_type=MESH
        )

    list_copy = pltpu.make_async_copy(lists_in, lists, list_sem.at[0])
    count_copy = pltpu.make_async_copy(counts_in, counts, list_sem.at[1])
    list_copy.start()
    count_copy.start()

    barrier = pltpu.get_barrier_semaphore()

    def hello(device):
        pl.semaphore_signal(barrier, inc=1, device_id=device, device_id_type=MESH)

    for dx, dy in OFFSETS:
        there = ((x + dx) % 4, (y + dy) % 4)
        if (dx, dy) != (0, 0):
            hello(at(z, *there, c))
        hello(at(z, *there, 1 - c))
    up = either(c == 0, not_last)
    down = either(c == 1, not_first)

    @pl.when(both(c == 0, not_first))
    def _():
        hello(at(z - 1, x, y, 1))

    @pl.when(both(c == 1, not_last))
    def _():
        hello(at(z + 1, x, y, 0))

    pl.semaphore_wait(
        barrier,
        31 + jnp.where(both(c == 1, not_last), 1, 0) + jnp.where(both(c == 0, not_first), 1, 0),
    )

    e = b % 2

    def scatter(r, source, target, row, size, s, sem):
        for dx, dy in OFFSETS:
            px, py = (x + dx) % 4, (y + dy) % 4
            src = source.at[:, columns((px * 4 + py) * 2 + r)]
            dst = target.at[rows(row, size), :]

            def away():
                remote(src, dst, send.at[s], sem, at(z, px, py, xl)).start()

            if (dx, dy) != (0, 0):
                away()
            else:
                @pl.when(mine)
                def _():
                    pltpu.make_async_copy(src, dst, sem).start()

                @pl.when(no(mine))
                def _():
                    away()

    def scatter_shared(source, target, row, size, s, sem):
        for dx, dp in PAIR_OFFSETS:
            px, pp = (x + dx) % 4, (y // 2 + dp) % 2
            src = source.at[:, columns(MAIN + px * 2 + pp)]
            dst = target.at[rows(row, size), :]

            def away():
                remote(src, dst, send.at[s], sem, at(z, px, pp * 2 + (xl + z) % 2, e)).start()

            if (dx, dp) != (0, 0):
                away()
            else:
                @pl.when(mine_l)
                def _():
                    pltpu.make_async_copy(src, dst, sem).start()

                @pl.when(no(mine_l))
                def _():
                    away()

    sends_prev, sends_next = b == 1, both(b == 2, u < 4)

    def scatter_halo(source, target, a):
        @pl.when(sends_prev)
        def _():
            for dx, dp in PAIR_OFFSETS:
                px, pp = (x + dx) % 4, (y // 2 + dp) % 2
                remote(
                    source.at[:, columns(MAIN + px * 2 + pp)], target.at[rows(u * KROWS, KROWS), :],
                    halo_send.at[a], halo_got.at[a], at(z, px, pp * 2 + (1 + z) % 2, 0),
                ).start()

        @pl.when(sends_next)
        def _():
            for dx, dp in PAIR_OFFSETS:
                px, pp = (x + dx) % 4, (y // 2 + dp) % 2
                remote(
                    source.at[:, columns(MAIN + px * 2 + pp)],
                    target.at[rows(2 * BLOCK + (u % 4) * KROWS, KROWS), :],
                    halo_send.at[a], halo_got.at[a], at(z, px, pp * 2 + z % 2, 1),
                ).start()

    kv_row, q_row = BLOCK * (1 + e) + u * KROWS, HALF * e + u * QROWS

    def send_k(r, target):
        scatter(r, k, target, kv_row, KROWS, 3 * r, got.at[4 * r + e])

    def send_v(r, target):
        scatter(r, v, target, kv_row, KROWS, 3 * r + 1, got.at[4 * r + 2 + e])

    def send_q(r, target):
        scatter(r, q, target, q_row, QROWS, 3 * r + 2, q_got.at[r])

    def halos(i, target):
        return (
            remote(
                target.at[pl.ds(2 * BLOCK, BLOCK), :], target.at[pl.ds(0, BLOCK), :],
                fwd_send.at[2 * i], fwd_got.at[2 * i], at(z + c, x, y, 1 - c),
            ),
            remote(
                target.at[pl.ds(BLOCK, HALF), :], target.at[pl.ds(3 * BLOCK, HALF), :],
                fwd_send.at[2 * i + 1], fwd_got.at[2 * i + 1], at(z - 1 + c, x, y, 1 - c),
            ),
        )

    def pass_on(i, target):
        to_up, to_down = halos(i, target)
        arrived(target.at[pl.ds(2 * BLOCK, BLOCK), :], got.at[2 * i + 1])
        arrived(target.at[pl.ds(BLOCK, BLOCK), :], got.at[2 * i])
        pl.when(c == 0)(to_up.start)
        pl.when(c == 1)(to_down.start)
        pl.when(both(c == 1, not_last))(to_up.start)
        pl.when(both(c == 0, not_first))(to_down.start)

    def near_in(i, target):
        to_up, to_down = halos(i, target)
        pl.when(c == 1)(to_up.wait_recv)
        pl.when(c == 0)(to_down.wait_recv)

    def far_in(i, target):
        to_up, to_down = halos(i, target)
        pl.when(both(c == 0, not_first))(to_up.wait_recv)
        pl.when(both(c == 1, not_last))(to_down.wait_recv)

    def halos_sent(i, target):
        to_up, to_down = halos(i, target)

        @pl.when(up)
        def _():
            to_up.wait_send()

        @pl.when(down)
        def _():
            to_down.wait_send()

    def shared_copies(a, target):
        block, half = target.at[pl.ds(BLOCK, BLOCK), :], target.at[pl.ds(BLOCK, HALF), :]
        prev, after = target.at[pl.ds(0, BLOCK), :], target.at[pl.ds(2 * BLOCK, HALF), :]
        near, far = (fwd_send.at[8 + a], fwd_got.at[8 + a]), (fwd_send.at[10 + a], fwd_got.at[10 + a])
        return (
            (c == 0, c == 1, remote(block, prev, *near, at(z, x, y, 1))),
            (c == 1, c == 0, remote(half, after, *near, at(z, x, y, 0))),
            (both(quarter == 3, not_last), both(quarter == 0, not_first), remote(block, prev, *far, at(z + 1, x, y, 0))),
            (both(quarter == 0, not_first), both(quarter == 3, not_last), remote(half, after, *far, at(z - 1, x, y, 1))),
        )

    def own_shared(a, target):
        arrived(target.at[pl.ds(BLOCK, BLOCK), :], got.at[8 + a])

    def relay(a, target):
        @pl.when(outer)
        def _():
            own_shared(a, target)
            for sends, _, copy in shared_copies(a, target)[2:]:
                pl.when(sends)(copy.start)

    def share(a, target):
        @pl.when(no(outer))
        def _():
            own_shared(a, target)

        for sends, _, copy in shared_copies(a, target)[:2]:
            pl.when(sends)(copy.start)

    def shared_in(a, target):
        @pl.when(quarter == 2)
        def _():
            arrived(target.at[pl.ds(0, BLOCK), :], halo_got.at[a])

        @pl.when(quarter == 1)
        def _():
            arrived(target.at[pl.ds(2 * BLOCK, HALF), :], halo_got.at[a])

        for sends, gets, copy in shared_copies(a, target):
            pl.when(sends)(copy.wait_send)
            pl.when(gets)(copy.wait_recv)

    def lay_out(keys, values, start, stop):
        def one(t, carry):
            row = pl.ds(pl.multiple_of(t * TILE, TILE), TILE)
            if keys is not None:
                kt[t] = keys[row, :]
            if values is not None:
                vt[t, 0:HD, :] = values[row, :].T
            return carry

        lax.fori_loop(start, stop, one, 0)

    def attend(queries, query_row, block, first_block, done_row, tiles):
        def scale(t, carry):
            row = pl.multiple_of(query_row + t * TILE, TILE)
            query = queries[pl.ds(row, TILE), :].astype(jnp.float32).T * LOG2_SCALE
            high = query.astype(jnp.bfloat16)
            qt[t, 0:HD, :] = high
            qt[t, HD:2 * HD, :] = (query - high.astype(jnp.float32)).astype(jnp.bfloat16)
            return carry

        first = first_block * 6

        def place(tile, m):
            return jnp.clip(lists[tile, m] - first, 0, tiles - 1)

        def scores(buffer, t, g):
            tile = block * FT + t
            top = None
            for j in range(G):
                key = kt[place(tile, g * G + j)]
                s = jnp.dot(jnp.concatenate([key, key], axis=1), qt[t], preferred_element_type=jnp.float32)
                buffer[j * TILE:(j + 1) * TILE, :] = s
                t_top = jnp.max(s, axis=0, keepdims=True)
                top = t_top if top is None else jnp.maximum(top, t_top)
            return top

        def weigh(buffer, t, g, peak):
            tile = block * FT + t
            total = None
            for j in range(G):
                m = g * G + j
                shift = peak + jnp.maximum(m + 1 - counts[tile], 0).astype(jnp.float32) * FAR
                w = jnp.exp2(buffer[j * TILE:(j + 1) * TILE, :] - shift).astype(jnp.bfloat16)
                part = jnp.dot(vt[place(tile, m)], w, preferred_element_type=jnp.float32)
                total = part if total is None else total + part
            return total

        def put(t):
            total = acc[...]
            row = pl.multiple_of(done_row + t * TILE, TILE)
            done[pl.ds(row, TILE), :] = (total[:HD] / total[HD:HD + 1]).T.astype(jnp.bfloat16)

        def query_tile(t, peak):
            acc[...] = jnp.zeros_like(acc)

            def step(i, peak):
                g = 2 * i
                top = scores(s1, t, g + 1)
                part = weigh(s0, t, g, peak)
                higher = jnp.maximum(peak, top)
                acc[...] = (acc[...] + part) * jnp.exp2(peak - higher)
                after = jnp.where(g + 2 < GROUPS, 0, 1)
                top = scores(s0, jnp.minimum(t + after, FT - 1), (g + 2) * (1 - after))
                part = weigh(s1, t, g + 1, higher)
                highest = jnp.where(after == 1, top, jnp.maximum(higher, top))
                acc[...] = (acc[...] + part) * jnp.where(after == 1, 1.0, jnp.exp2(higher - highest))
                return highest

            peak = lax.fori_loop(0, GROUPS // 2, step, peak)
            put(t)
            return peak

        def all_tiles():
            lax.fori_loop(0, FT, scale, 0)
            lax.fori_loop(0, FT, query_tile, scores(s0, 0, 0))

        def keep(t, carry):
            def step(g, peak):
                return jnp.maximum(peak, scores(kept.at[t * GROUPS + g], t, g))

            peaks[t] = lax.fori_loop(0, GROUPS, step, jnp.full((1, TILE), -FAR, jnp.float32))
            return carry

        def finish(t, carry):
            peak = peaks[t]
            acc[...] = jnp.zeros_like(acc)

            def step(i, carry):
                g = 2 * i
                part = weigh(kept.at[t * GROUPS + g], t, g, peak)
                acc[...] += part + weigh(kept.at[t * GROUPS + g + 1], t, g + 1, peak)
                return carry

            lax.fori_loop(0, GROUPS // 2, step, 0)
            put(t)
            return carry

        def first_stage():
            lax.fori_loop(0, FT, scale, 0)
            lax.fori_loop(0, FT, keep, 0)

        def second_stage():
            lax.fori_loop(0, FT, finish, 0)

        return all_tiles, first_stage, second_stage

    def give_back(done_row, head, half, core, local, s):
        for dh, dy in HALF_OFFSETS:
            px, py = (x // 2 * 2 + 2 * dh + half) % 4, (y + dy) % 4
            src = done.at[rows(done_row + ((px // 2) * 4 + py) * QROWS, QROWS), :]
            dst = out.at[:, columns(head)]

            def away():
                remote(src, dst, out_send.at[s], out_got, at(z, px, py, core)).start()

            if (dh, dy) != (0, 0):
                away()
            else:
                @pl.when(local)
                def _():
                    pltpu.make_async_copy(src, dst, out_got).start()

                @pl.when(no(local))
                def _():
                    away()

    def unit(queries, r, e):
        return attend(
            queries, e * HALF, 4 * z + 2 * c + e, 4 * z + 2 * c - 1, (2 * r + e) * HALF, PAIR // TILE
        )

    def return_unit(r, e):
        give_back((2 * r + e) * HALF, chip * 2 + r, c, e, both(mine, c == e), r)

    inner_e, outer_e = 1 - c, c
    near_tiles = (jnp.where(c == 0, 6, 0), jnp.where(c == 0, 21, 18))
    far_tiles = (jnp.where(c == 0, 0, 18), jnp.where(c == 0, 6, 21))
    send_q(0, qa)
    send_k(0, ka)
    send_v(0, va)
    vt[:, HD:VROWS, :] = jnp.ones((vt.shape[0], VROWS - HD, TILE), jnp.bfloat16)
    list_copy.wait()
    count_copy.wait()
    pass_on(0, ka)
    send_q(1, qb)
    pass_on(1, va)
    send_k(1, kb)
    send_v(1, vb)
    arrived(qa, q_got.at[0])
    near_in(0, ka)
    near_in(1, va)
    lay_out(ka, va, *near_tiles)
    unit(qa, 0, inner_e)[0]()
    pass_on(2, kb)
    scatter_shared(q, ql, u * QROWS, QROWS, 8, q_got.at[2])
    scatter_shared(k, kl, BLOCK + u * KROWS, KROWS, 6, got.at[8])
    scatter_halo(k, kl, 0)
    far_in(0, ka)
    far_in(1, va)
    lay_out(ka, va, *far_tiles)
    unit(qa, 0, outer_e)[0]()
    pass_on(3, vb)
    scatter_shared(v, vl, BLOCK + u * KROWS, KROWS, 7, got.at[9])
    scatter_halo(v, vl, 1)
    arrived(qb, q_got.at[1])
    near_in(2, kb)
    lay_out(kb, None, *near_tiles)
    _, first_stage, second_stage = unit(qb, 1, inner_e)
    first_stage()
    near_in(3, vb)
    lay_out(None, vb, *near_tiles)
    second_stage()
    relay(0, kl)
    share(0, kl)
    return_unit(0, inner_e)
    return_unit(0, outer_e)
    return_unit(1, inner_e)
    far_in(2, kb)
    far_in(3, vb)
    lay_out(kb, vb, *far_tiles)
    unit(qb, 1, outer_e)[0]()
    relay(1, vl)
    share(1, vl)
    return_unit(1, outer_e)
    arrived(ql, q_got.at[2])
    shared_in(0, kl)
    lay_out(kl, None, 0, ONE // TILE)
    _, first_stage, second_stage = attend(
        ql, 0, 4 * z + quarter, 4 * z + quarter - 1, 4 * HALF, ONE // TILE
    )
    first_stage()
    shared_in(1, vl)
    lay_out(None, vl, 0, ONE // TILE)
    second_stage()
    give_back(4 * HALF, MAIN + chip // 2, side, c, mine_l, 2)

    for i, target in enumerate((ka, va, kb, vb)):
        halos_sent(i, target)

    def sent(source, many, fewer, n, sem):
        for condition, size in ((fewer, n - 1), (no(fewer), n)):
            @pl.when(condition)
            def _():
                arrived(many(source, size), sem)

    def heads(source, n):
        return source.at[:, pl.ds(0, n * HD)]

    def parts(source, n):
        return source.at[pl.ds(0, n * QROWS), :]

    for a, source in enumerate((k, v, q)):
        sent(source, heads, mine, 16, send.at[a])
        sent(source, heads, mine, 16, send.at[3 + a])
        sent(source, heads, mine_l, 8, send.at[6 + a])
    for a, source in enumerate((k, v)):
        @pl.when(either(sends_prev, sends_next))
        def _():
            arrived(heads(source, 8), halo_send.at[a])
    sent(done, parts, mine, 16, out_send.at[0])
    sent(done, parts, mine, 16, out_send.at[1])
    sent(done, parts, mine_l, 8, out_send.at[2])
    arrived(out, out_got)


def per_device(queries, keys, values, tile_lists, tile_counts):
    anywhere = pl.BlockSpec(memory_space=pl.ANY)
    far = pl.BlockSpec(memory_space=pltpu.HBM)
    dma = pltpu.SemaphoreType.DMA

    def held(n):
        return pltpu.VMEM((n, HD), jnp.bfloat16)

    return pl.pallas_call(
        kernel,
        out_shape=jax.ShapeDtypeStruct((QROWS, HEADS * HD), jnp.bfloat16),
        in_specs=[far] * 5,
        out_specs=anywhere,
        scratch_shapes=[
            pltpu.SMEM(tile_lists.shape, jnp.int32), pltpu.SMEM(tile_counts.shape, jnp.int32), dma((2,)),
            held(2 * HALF), held(2 * HALF), held(HALF),
            held(PAIR), held(PAIR), held(ONE),
            held(PAIR), held(PAIR), held(ONE),
            held(5 * HALF),
            pltpu.VMEM((PAIR // TILE, TILE, HD), jnp.bfloat16),
            pltpu.VMEM((PAIR // TILE, VROWS, TILE), jnp.bfloat16),
            pltpu.VMEM((FT, 2 * HD, TILE), jnp.bfloat16),
            pltpu.VMEM((G * TILE, TILE), jnp.float32),
            pltpu.VMEM((G * TILE, TILE), jnp.float32),
            pltpu.VMEM((VROWS, TILE), jnp.float32),
            pltpu.VMEM((FT * GROUPS, G * TILE, TILE), jnp.float32),
            pltpu.VMEM((FT, 1, TILE), jnp.float32),
            dma((9,)), dma((10,)), dma((3,)), dma((12,)), dma((12,)), dma((2,)), dma((2,)), dma((3,)), dma,
        ],
        compiler_params=pltpu.CompilerParams(
            collective_id=0, has_side_effects=True, vmem_limit_bytes=54 * 1024 * 1024
        ),
        name="attention",
    )(tile_lists, tile_counts, queries, keys, values)


def solution(mesh):
    placed = (P(("blk", "uly"), None), P(("blk", "uly"), None), P(("blk", "uly"), None), P(), P())
    return jax.shard_map(
        per_device, mesh=mesh, in_specs=placed, out_specs=P(("blk", "uly"), None), check_vma=False
    )
```

```python
import functools

import jax
import jax.numpy as jnp
from jax import lax
from jax.experimental import pallas as pl
from jax.experimental.pallas import tpu as pltpu
from jax.sharding import PartitionSpec as P

HD = 128
TILE = 384
FT = 3
MAXT = 12
HEADS = 40
BLOCK = 2304
HALF = 1152
KROWS = 288
QROWS = 144
MAIN = 32
PAIR = 3 * BLOCK + HALF
ONE = 2 * BLOCK + HALF
VROWS = HD + 16
G = 6
GROUPS = MAXT // G
LOG2_SCALE = HD ** (-0.5) * 1.4426950408889634
FAR = 1e30
MESH = pl.DeviceIdType.MESH
OFFSETS = [(dx, (k - dx) % 4) for k in (1, 3, 2, 0) for dx in (1, 3, 2, 0)]
PAIR_OFFSETS = ((1, 0), (2, 1), (3, 0), (0, 1), (1, 1), (2, 0), (3, 1), (0, 0))
HALF_OFFSETS = ((0, 1), (1, 3), (1, 2), (0, 3), (1, 1), (0, 2), (1, 0), (0, 0))


def rows(start, size):
    return pl.ds(pl.multiple_of(start, 16), size)


def columns(head):
    return pl.ds(pl.multiple_of(head * HD, HD), HD)


def arrived(ref, sem):
    pltpu.make_async_copy(ref, ref, sem).wait()


def kernel(
    lists_in, counts_in, q, k, v, out,
    lists, counts, list_sem, qa, qb, ql, ka, kb, kl, va, vb, vl, done, kt, vt, qt, s0, s1, acc, kept, peaks,
    send, got, q_got, fwd_send, fwd_got, halo_send, halo_got, out_send, out_got,
):
    blk, u = lax.axis_index("blk"), lax.axis_index("uly")
    z, b, c = blk // 4, blk % 4, blk % 2
    xl = b // 2
    x, y = (u // 4) * 2 + xl, u % 4
    chip = x * 4 + y
    side = (y + z) % 2
    quarter = side * 2 + c
    outer = jnp.logical_or(quarter == 0, quarter == 3)
    not_first, not_last = z > 0, z < 3
    mine = xl == c
    mine_l = xl == side
    no = jnp.logical_not
    both = jnp.logical_and
    either = jnp.logical_or

    def at(z, x, y, c):
        return (z * 4 + (x % 2) * 2 + c, (x // 2) * 4 + y)

    def remote(src, dst, send_sem, recv_sem, device):
        return pltpu.make_async_remote_copy(
            src, dst, send_sem, recv_sem, device_id=device, device_id_type=MESH
        )

    list_copy = pltpu.make_async_copy(lists_in, lists, list_sem.at[0])
    count_copy = pltpu.make_async_copy(counts_in, counts, list_sem.at[1])
    list_copy.start()
    count_copy.start()

    barrier = pltpu.get_barrier_semaphore()

    def hello(device):
        pl.semaphore_signal(barrier, inc=1, device_id=device, device_id_type=MESH)

    for dx, dy in OFFSETS:
        there = ((x + dx) % 4, (y + dy) % 4)
        if (dx, dy) != (0, 0):
            hello(at(z, *there, c))
        hello(at(z, *there, 1 - c))
    up = either(c == 0, not_last)
    down = either(c == 1, not_first)

    @pl.when(both(c == 0, not_first))
    def _():
        hello(at(z - 1, x, y, 1))

    @pl.when(both(c == 1, not_last))
    def _():
        hello(at(z + 1, x, y, 0))

    pl.semaphore_wait(
        barrier,
        31 + jnp.where(both(c == 1, not_last), 1, 0) + jnp.where(both(c == 0, not_first), 1, 0),
    )

    e = b % 2

    def scatter(r, source, target, row, size, s, sem):
        for dx, dy in OFFSETS:
            px, py = (x + dx) % 4, (y + dy) % 4
            src = source.at[:, columns((px * 4 + py) * 2 + r)]
            dst = target.at[rows(row, size), :]

            def away():
                remote(src, dst, send.at[s], sem, at(z, px, py, xl)).start()

            if (dx, dy) != (0, 0):
                away()
            else:
                @pl.when(mine)
                def _():
                    pltpu.make_async_copy(src, dst, sem).start()

                @pl.when(no(mine))
                def _():
                    away()

    def scatter_shared(source, target, row, size, s, sem):
        for dx, dp in PAIR_OFFSETS:
            px, pp = (x + dx) % 4, (y // 2 + dp) % 2
            src = source.at[:, columns(MAIN + px * 2 + pp)]
            dst = target.at[rows(row, size), :]

            def away():
                remote(src, dst, send.at[s], sem, at(z, px, pp * 2 + (xl + z) % 2, e)).start()

            if (dx, dp) != (0, 0):
                away()
            else:
                @pl.when(mine_l)
                def _():
                    pltpu.make_async_copy(src, dst, sem).start()

                @pl.when(no(mine_l))
                def _():
                    away()

    sends_prev, sends_next = b == 1, both(b == 2, u < 4)

    def scatter_halo(source, target, a):
        @pl.when(sends_prev)
        def _():
            for dx, dp in PAIR_OFFSETS:
                px, pp = (x + dx) % 4, (y // 2 + dp) % 2
                remote(
                    source.at[:, columns(MAIN + px * 2 + pp)], target.at[rows(u * KROWS, KROWS), :],
                    halo_send.at[a], halo_got.at[a], at(z, px, pp * 2 + (1 + z) % 2, 0),
                ).start()

        @pl.when(sends_next)
        def _():
            for dx, dp in PAIR_OFFSETS:
                px, pp = (x + dx) % 4, (y // 2 + dp) % 2
                remote(
                    source.at[:, columns(MAIN + px * 2 + pp)],
                    target.at[rows(2 * BLOCK + (u % 4) * KROWS, KROWS), :],
                    halo_send.at[a], halo_got.at[a], at(z, px, pp * 2 + z % 2, 1),
                ).start()

    kv_row, q_row = BLOCK * (1 + e) + u * KROWS, HALF * e + u * QROWS

    def send_k(r, target):
        scatter(r, k, target, kv_row, KROWS, 3 * r, got.at[4 * r + e])

    def send_v(r, target):
        scatter(r, v, target, kv_row, KROWS, 3 * r + 1, got.at[4 * r + 2 + e])

    def send_q(r, target):
        scatter(r, q, target, q_row, QROWS, 3 * r + 2, q_got.at[r])

    def halos(i, target):
        return (
            remote(
                target.at[pl.ds(2 * BLOCK, BLOCK), :], target.at[pl.ds(0, BLOCK), :],
                fwd_send.at[2 * i], fwd_got.at[2 * i], at(z + c, x, y, 1 - c),
            ),
            remote(
                target.at[pl.ds(BLOCK, HALF), :], target.at[pl.ds(3 * BLOCK, HALF), :],
                fwd_send.at[2 * i + 1], fwd_got.at[2 * i + 1], at(z - 1 + c, x, y, 1 - c),
            ),
        )

    def pass_on(i, target):
        to_up, to_down = halos(i, target)
        arrived(target.at[pl.ds(2 * BLOCK, BLOCK), :], got.at[2 * i + 1])
        arrived(target.at[pl.ds(BLOCK, BLOCK), :], got.at[2 * i])
        pl.when(c == 0)(to_up.start)
        pl.when(c == 1)(to_down.start)
        pl.when(both(c == 1, not_last))(to_up.start)
        pl.when(both(c == 0, not_first))(to_down.start)

    def near_in(i, target):
        to_up, to_down = halos(i, target)
        pl.when(c == 1)(to_up.wait_recv)
        pl.when(c == 0)(to_down.wait_recv)

    def far_in(i, target):
        to_up, to_down = halos(i, target)
        pl.when(both(c == 0, not_first))(to_up.wait_recv)
        pl.when(both(c == 1, not_last))(to_down.wait_recv)

    def halos_sent(i, target):
        to_up, to_down = halos(i, target)

        @pl.when(up)
        def _():
            to_up.wait_send()

        @pl.when(down)
        def _():
            to_down.wait_send()

    def shared_copies(a, target):
        block, half = target.at[pl.ds(BLOCK, BLOCK), :], target.at[pl.ds(BLOCK, HALF), :]
        prev, after = target.at[pl.ds(0, BLOCK), :], target.at[pl.ds(2 * BLOCK, HALF), :]
        near, far = (fwd_send.at[8 + a], fwd_got.at[8 + a]), (fwd_send.at[10 + a], fwd_got.at[10 + a])
        return (
            (c == 0, c == 1, remote(block, prev, *near, at(z, x, y, 1))),
            (c == 1, c == 0, remote(half, after, *near, at(z, x, y, 0))),
            (both(quarter == 3, not_last), both(quarter == 0, not_first), remote(block, prev, *far, at(z + 1, x, y, 0))),
            (both(quarter == 0, not_first), both(quarter == 3, not_last), remote(half, after, *far, at(z - 1, x, y, 1))),
        )

    def own_shared(a, target):
        arrived(target.at[pl.ds(BLOCK, BLOCK), :], got.at[8 + a])

    def relay(a, target):
        @pl.when(outer)
        def _():
            own_shared(a, target)
            for sends, _, copy in shared_copies(a, target)[2:]:
                pl.when(sends)(copy.start)

    def share(a, target):
        @pl.when(no(outer))
        def _():
            own_shared(a, target)

        for sends, _, copy in shared_copies(a, target)[:2]:
            pl.when(sends)(copy.start)

    def shared_in(a, target):
        @pl.when(quarter == 2)
        def _():
            arrived(target.at[pl.ds(0, BLOCK), :], halo_got.at[a])

        @pl.when(quarter == 1)
        def _():
            arrived(target.at[pl.ds(2 * BLOCK, HALF), :], halo_got.at[a])

        for sends, gets, copy in shared_copies(a, target):
            pl.when(sends)(copy.wait_send)
            pl.when(gets)(copy.wait_recv)

    def lay_out(keys, values, start, stop):
        def one(t, carry):
            row = pl.ds(pl.multiple_of(t * TILE, TILE), TILE)
            if keys is not None:
                kt[t] = keys[row, :]
            if values is not None:
                vt[t, 0:HD, :] = values[row, :].T
            return carry

        lax.fori_loop(start, stop, one, 0)

    def attend(queries, query_row, block, first_block, done_row, tiles):
        def scale(t, carry):
            row = pl.multiple_of(query_row + t * TILE, TILE)
            query = queries[pl.ds(row, TILE), :].astype(jnp.float32).T * LOG2_SCALE
            high = query.astype(jnp.bfloat16)
            qt[t, 0:HD, :] = high
            qt[t, HD:2 * HD, :] = (query - high.astype(jnp.float32)).astype(jnp.bfloat16)
            return carry

        first = first_block * 6

        def place(tile, m):
            return jnp.clip(lists[m, tile] - first, 0, tiles - 1)

        def scores(buffer, t, g):
            tile = block * FT + t
            top = None
            for j in range(G):
                key = kt[place(tile, g * G + j)]
                s = jnp.dot(jnp.concatenate([key, key], axis=1), qt[t], preferred_element_type=jnp.float32)
                buffer[j * TILE:(j + 1) * TILE, :] = s
                t_top = jnp.max(s, axis=0, keepdims=True)
                top = t_top if top is None else jnp.maximum(top, t_top)
            return top

        def weigh(buffer, t, g, peak):
            tile = block * FT + t
            total = None
            for j in range(G):
                m = g * G + j
                shift = peak + jnp.maximum(m + 1 - counts[tile], 0).astype(jnp.float32) * FAR
                w = jnp.exp2(buffer[j * TILE:(j + 1) * TILE, :] - shift).astype(jnp.bfloat16)
                part = jnp.dot(vt[place(tile, m)], w, preferred_element_type=jnp.float32)
                total = part if total is None else total + part
            return total

        def put(t):
            total = acc[...]
            row = pl.multiple_of(done_row + t * TILE, TILE)
            done[pl.ds(row, TILE), :] = (total[:HD] / total[HD:HD + 1]).T.astype(jnp.bfloat16)

        def query_tile(t, peak):
            acc[...] = jnp.zeros_like(acc)

            def step(i, peak):
                g = 2 * i
                top = scores(s1, t, g + 1)
                part = weigh(s0, t, g, peak)
                higher = jnp.maximum(peak, top)
                acc[...] = (acc[...] + part) * jnp.exp2(peak - higher)
                after = jnp.where(g + 2 < GROUPS, 0, 1)
                top = scores(s0, jnp.minimum(t + after, FT - 1), (g + 2) * (1 - after))
                part = weigh(s1, t, g + 1, higher)
                highest = jnp.where(after == 1, top, jnp.maximum(higher, top))
                acc[...] = (acc[...] + part) * jnp.where(after == 1, 1.0, jnp.exp2(higher - highest))
                return highest

            peak = lax.fori_loop(0, GROUPS // 2, step, peak)
            put(t)
            return peak

        def all_tiles():
            lax.fori_loop(0, FT, scale, 0)
            lax.fori_loop(0, FT, query_tile, scores(s0, 0, 0))

        def keep(t, carry):
            def step(g, peak):
                return jnp.maximum(peak, scores(kept.at[t * GROUPS + g], t, g))

            peaks[t] = lax.fori_loop(0, GROUPS, step, jnp.full((1, TILE), -FAR, jnp.float32))
            return carry

        def finish(t, carry):
            peak = peaks[t]
            acc[...] = jnp.zeros_like(acc)

            def step(i, carry):
                g = 2 * i
                part = weigh(kept.at[t * GROUPS + g], t, g, peak)
                acc[...] += part + weigh(kept.at[t * GROUPS + g + 1], t, g + 1, peak)
                return carry

            lax.fori_loop(0, GROUPS // 2, step, 0)
            put(t)
            return carry

        def first_stage():
            lax.fori_loop(0, FT, scale, 0)
            lax.fori_loop(0, FT, keep, 0)

        def second_stage():
            lax.fori_loop(0, FT, finish, 0)

        return all_tiles, first_stage, second_stage

    def give_back(done_row, head, half, core, local, s):
        for dh, dy in HALF_OFFSETS:
            px, py = (x // 2 * 2 + 2 * dh + half) % 4, (y + dy) % 4
            src = done.at[rows(done_row + ((px // 2) * 4 + py) * QROWS, QROWS), :]
            dst = out.at[:, columns(head)]

            def away():
                remote(src, dst, out_send.at[s], out_got, at(z, px, py, core)).start()

            if (dh, dy) != (0, 0):
                away()
            else:
                @pl.when(local)
                def _():
                    pltpu.make_async_copy(src, dst, out_got).start()

                @pl.when(no(local))
                def _():
                    away()

    def unit(queries, r, e):
        return attend(
            queries, e * HALF, 4 * z + 2 * c + e, 4 * z + 2 * c - 1, (2 * r + e) * HALF, PAIR // TILE
        )

    def return_unit(r, e):
        give_back((2 * r + e) * HALF, chip * 2 + r, c, e, both(mine, c == e), r)

    inner_e, outer_e = 1 - c, c
    near_tiles = (jnp.where(c == 0, 6, 0), jnp.where(c == 0, 21, 18))
    far_tiles = (jnp.where(c == 0, 0, 18), jnp.where(c == 0, 6, 21))
    send_q(0, qa)
    send_k(0, ka)
    send_v(0, va)
    vt[:, HD:VROWS, :] = jnp.ones((vt.shape[0], VROWS - HD, TILE), jnp.bfloat16)
    list_copy.wait()
    count_copy.wait()
    pass_on(0, ka)
    send_q(1, qb)
    pass_on(1, va)
    send_k(1, kb)
    send_v(1, vb)
    scatter_shared(q, ql, u * QROWS, QROWS, 8, q_got.at[2])
    scatter_shared(k, kl, BLOCK + u * KROWS, KROWS, 6, got.at[8])
    scatter_halo(k, kl, 0)
    arrived(qa, q_got.at[0])
    near_in(0, ka)
    near_in(1, va)
    lay_out(ka, va, *near_tiles)
    unit(qa, 0, inner_e)[0]()
    pass_on(2, kb)
    far_in(0, ka)
    far_in(1, va)
    lay_out(ka, va, *far_tiles)
    unit(qa, 0, outer_e)[0]()
    pass_on(3, vb)
    scatter_shared(v, vl, BLOCK + u * KROWS, KROWS, 7, got.at[9])
    scatter_halo(v, vl, 1)
    arrived(qb, q_got.at[1])
    near_in(2, kb)
    lay_out(kb, None, *near_tiles)
    _, first_stage, second_stage = unit(qb, 1, inner_e)
    first_stage()
    near_in(3, vb)
    lay_out(None, vb, *near_tiles)
    second_stage()
    relay(0, kl)
    share(0, kl)
    return_unit(0, inner_e)
    return_unit(0, outer_e)
    return_unit(1, inner_e)
    far_in(2, kb)
    far_in(3, vb)
    lay_out(kb, vb, *far_tiles)
    unit(qb, 1, outer_e)[0]()
    relay(1, vl)
    share(1, vl)
    return_unit(1, outer_e)
    arrived(ql, q_got.at[2])
    shared_in(0, kl)
    lay_out(kl, None, 0, ONE // TILE)
    _, first_stage, second_stage = attend(
        ql, 0, 4 * z + quarter, 4 * z + quarter - 1, 4 * HALF, ONE // TILE
    )
    first_stage()
    shared_in(1, vl)
    lay_out(None, vl, 0, ONE // TILE)
    second_stage()
    give_back(4 * HALF, MAIN + chip // 2, side, c, mine_l, 2)

    for i, target in enumerate((ka, va, kb, vb)):
        halos_sent(i, target)

    def sent(source, many, fewer, n, sem):
        for condition, size in ((fewer, n - 1), (no(fewer), n)):
            @pl.when(condition)
            def _():
                arrived(many(source, size), sem)

    def heads(source, n):
        return source.at[:, pl.ds(0, n * HD)]

    def parts(source, n):
        return source.at[pl.ds(0, n * QROWS), :]

    for a, source in enumerate((k, v, q)):
        sent(source, heads, mine, 16, send.at[a])
        sent(source, heads, mine, 16, send.at[3 + a])
        sent(source, heads, mine_l, 8, send.at[6 + a])
    for a, source in enumerate((k, v)):
        @pl.when(either(sends_prev, sends_next))
        def _():
            arrived(heads(source, 8), halo_send.at[a])
    sent(done, parts, mine, 16, out_send.at[0])
    sent(done, parts, mine, 16, out_send.at[1])
    sent(done, parts, mine_l, 8, out_send.at[2])
    arrived(out, out_got)


def per_device(queries, keys, values, tile_lists, tile_counts):
    anywhere = pl.BlockSpec(memory_space=pl.ANY)
    far = pl.BlockSpec(memory_space=pltpu.HBM)
    dma = pltpu.SemaphoreType.DMA

    def held(n):
        return pltpu.VMEM((n, HD), jnp.bfloat16)

    return pl.pallas_call(
        kernel,
        out_shape=jax.ShapeDtypeStruct((QROWS, HEADS * HD), jnp.bfloat16),
        in_specs=[far] * 5,
        out_specs=anywhere,
        scratch_shapes=[
            pltpu.SMEM(tile_lists.shape[::-1], jnp.int32), pltpu.SMEM(tile_counts.shape, jnp.int32), dma((2,)),
            held(2 * HALF), held(2 * HALF), held(HALF),
            held(PAIR), held(PAIR), held(ONE),
            held(PAIR), held(PAIR), held(ONE),
            held(5 * HALF),
            pltpu.VMEM((PAIR // TILE, TILE, HD), jnp.bfloat16),
            pltpu.VMEM((PAIR // TILE, VROWS, TILE), jnp.bfloat16),
            pltpu.VMEM((FT, 2 * HD, TILE), jnp.bfloat16),
            pltpu.VMEM((G * TILE, TILE), jnp.float32),
            pltpu.VMEM((G * TILE, TILE), jnp.float32),
            pltpu.VMEM((VROWS, TILE), jnp.float32),
            pltpu.VMEM((FT * GROUPS, G * TILE, TILE), jnp.float32),
            pltpu.VMEM((FT, 1, TILE), jnp.float32),
            dma((9,)), dma((10,)), dma((3,)), dma((12,)), dma((12,)), dma((2,)), dma((2,)), dma((3,)), dma,
        ],
        compiler_params=pltpu.CompilerParams(
            collective_id=0, has_side_effects=True, vmem_limit_bytes=52 * 1024 * 1024
        ),
        name="attention",
    )(tile_lists.T, tile_counts, queries, keys, values)


def solution(mesh):
    placed = (P(("blk", "uly"), None), P(("blk", "uly"), None), P(("blk", "uly"), None), P(), P())
    return jax.shard_map(
        per_device, mesh=mesh, in_specs=placed, out_specs=P(("blk", "uly"), None), check_vma=False
    )
```

```python
import functools

import jax
import jax.numpy as jnp
from jax import lax
from jax.experimental import pallas as pl
from jax.experimental.pallas import tpu as pltpu
from jax.sharding import PartitionSpec as P

HD = 128
TILE = 384
FT = 3
MAXT = 12
HEADS = 40
BLOCK = 2304
HALF = 1152
KROWS = 288
QROWS = 144
MAIN = 32
PAIR = 3 * BLOCK + HALF
ONE = 2 * BLOCK + HALF
VROWS = HD + 16
G = 6
GROUPS = MAXT // G
LOG2_SCALE = HD ** (-0.5) * 1.4426950408889634
FAR = 1e30
MESH = pl.DeviceIdType.MESH
OFFSETS = [(dx, (k - dx) % 4) for k in (1, 3, 2, 0) for dx in (1, 3, 2, 0)]
PAIR_OFFSETS = ((1, 0), (2, 1), (3, 0), (0, 1), (1, 1), (2, 0), (3, 1), (0, 0))
HALF_OFFSETS = ((0, 1), (1, 3), (1, 2), (0, 3), (1, 1), (0, 2), (1, 0), (0, 0))


def rows(start, size):
    return pl.ds(pl.multiple_of(start, 16), size)


def columns(head):
    return pl.ds(pl.multiple_of(head * HD, HD), HD)


def arrived(ref, sem):
    pltpu.make_async_copy(ref, ref, sem).wait()


def kernel(
    lists_in, counts_in, q, k, v, out,
    lists, counts, list_sem, qa, qb, ql, ka, kb, kl, va, vb, vl, done, kt, vt, qt, s0, s1, acc, kept, peaks,
    send, got, q_got, fwd_send, fwd_got, halo_send, halo_got, out_send, out_got,
):
    blk, u = lax.axis_index("blk"), lax.axis_index("uly")
    z, b, c = blk // 4, blk % 4, blk % 2
    xl = b // 2
    x, y = (u // 4) * 2 + xl, u % 4
    chip = x * 4 + y
    side = (y + z) % 2
    quarter = side * 2 + c
    outer = jnp.logical_or(quarter == 0, quarter == 3)
    not_first, not_last = z > 0, z < 3
    mine = xl == c
    mine_l = xl == side
    no = jnp.logical_not
    both = jnp.logical_and
    either = jnp.logical_or

    def at(z, x, y, c):
        return (z * 4 + (x % 2) * 2 + c, (x // 2) * 4 + y)

    def remote(src, dst, send_sem, recv_sem, device):
        return pltpu.make_async_remote_copy(
            src, dst, send_sem, recv_sem, device_id=device, device_id_type=MESH
        )

    list_copy = pltpu.make_async_copy(lists_in, lists, list_sem.at[0])
    count_copy = pltpu.make_async_copy(counts_in, counts, list_sem.at[1])
    list_copy.start()
    count_copy.start()

    barrier = pltpu.get_barrier_semaphore()

    def hello(device):
        pl.semaphore_signal(barrier, inc=1, device_id=device, device_id_type=MESH)

    for dx, dy in OFFSETS:
        there = ((x + dx) % 4, (y + dy) % 4)
        if (dx, dy) != (0, 0):
            hello(at(z, *there, c))
        hello(at(z, *there, 1 - c))
    up = either(c == 0, not_last)
    down = either(c == 1, not_first)

    @pl.when(both(c == 0, not_first))
    def _():
        hello(at(z - 1, x, y, 1))

    @pl.when(both(c == 1, not_last))
    def _():
        hello(at(z + 1, x, y, 0))

    pl.semaphore_wait(
        barrier,
        31 + jnp.where(both(c == 1, not_last), 1, 0) + jnp.where(both(c == 0, not_first), 1, 0),
    )

    e = b % 2

    def scatter(r, source, target, row, size, s, sem):
        for dx, dy in OFFSETS:
            px, py = (x + dx) % 4, (y + dy) % 4
            src = source.at[:, columns((px * 4 + py) * 2 + r)]
            dst = target.at[rows(row, size), :]

            def away():
                remote(src, dst, send.at[s], sem, at(z, px, py, xl)).start()

            if (dx, dy) != (0, 0):
                away()
            else:
                @pl.when(mine)
                def _():
                    pltpu.make_async_copy(src, dst, sem).start()

                @pl.when(no(mine))
                def _():
                    away()

    def scatter_shared(source, target, row, size, s, sem):
        for dx, dp in PAIR_OFFSETS:
            px, pp = (x + dx) % 4, (y // 2 + dp) % 2
            src = source.at[:, columns(MAIN + px * 2 + pp)]
            dst = target.at[rows(row, size), :]

            def away():
                remote(src, dst, send.at[s], sem, at(z, px, pp * 2 + (xl + z) % 2, e)).start()

            if (dx, dp) != (0, 0):
                away()
            else:
                @pl.when(mine_l)
                def _():
                    pltpu.make_async_copy(src, dst, sem).start()

                @pl.when(no(mine_l))
                def _():
                    away()

    sends_prev, sends_next = b == 1, both(b == 2, u < 4)

    def scatter_halo(source, target, a):
        @pl.when(sends_prev)
        def _():
            for dx, dp in PAIR_OFFSETS:
                px, pp = (x + dx) % 4, (y // 2 + dp) % 2
                remote(
                    source.at[:, columns(MAIN + px * 2 + pp)], target.at[rows(u * KROWS, KROWS), :],
                    halo_send.at[a], halo_got.at[a], at(z, px, pp * 2 + (1 + z) % 2, 0),
                ).start()

        @pl.when(sends_next)
        def _():
            for dx, dp in PAIR_OFFSETS:
                px, pp = (x + dx) % 4, (y // 2 + dp) % 2
                remote(
                    source.at[:, columns(MAIN + px * 2 + pp)],
                    target.at[rows(2 * BLOCK + (u % 4) * KROWS, KROWS), :],
                    halo_send.at[a], halo_got.at[a], at(z, px, pp * 2 + z % 2, 1),
                ).start()

    kv_row, q_row = BLOCK * (1 + e) + u * KROWS, HALF * e + u * QROWS

    def send_k(r, target):
        scatter(r, k, target, kv_row, KROWS, 3 * r, got.at[4 * r + e])

    def send_v(r, target):
        scatter(r, v, target, kv_row, KROWS, 3 * r + 1, got.at[4 * r + 2 + e])

    def send_q(r, target):
        scatter(r, q, target, q_row, QROWS, 3 * r + 2, q_got.at[r])

    def halos(i, target):
        return (
            remote(
                target.at[pl.ds(2 * BLOCK, BLOCK), :], target.at[pl.ds(0, BLOCK), :],
                fwd_send.at[2 * i], fwd_got.at[2 * i], at(z + c, x, y, 1 - c),
            ),
            remote(
                target.at[pl.ds(BLOCK, HALF), :], target.at[pl.ds(3 * BLOCK, HALF), :],
                fwd_send.at[2 * i + 1], fwd_got.at[2 * i + 1], at(z - 1 + c, x, y, 1 - c),
            ),
        )

    def pass_on(i, target):
        to_up, to_down = halos(i, target)
        arrived(target.at[pl.ds(2 * BLOCK, BLOCK), :], got.at[2 * i + 1])
        arrived(target.at[pl.ds(BLOCK, BLOCK), :], got.at[2 * i])
        pl.when(c == 0)(to_up.start)
        pl.when(c == 1)(to_down.start)
        pl.when(both(c == 1, not_last))(to_up.start)
        pl.when(both(c == 0, not_first))(to_down.start)

    def near_in(i, target):
        to_up, to_down = halos(i, target)
        pl.when(c == 1)(to_up.wait_recv)
        pl.when(c == 0)(to_down.wait_recv)

    def far_in(i, target):
        to_up, to_down = halos(i, target)
        pl.when(both(c == 0, not_first))(to_up.wait_recv)
        pl.when(both(c == 1, not_last))(to_down.wait_recv)

    def halos_sent(i, target):
        to_up, to_down = halos(i, target)

        @pl.when(up)
        def _():
            to_up.wait_send()

        @pl.when(down)
        def _():
            to_down.wait_send()

    def shared_copies(a, target):
        block, half = target.at[pl.ds(BLOCK, BLOCK), :], target.at[pl.ds(BLOCK, HALF), :]
        prev, after = target.at[pl.ds(0, BLOCK), :], target.at[pl.ds(2 * BLOCK, HALF), :]
        near, far = (fwd_send.at[8 + a], fwd_got.at[8 + a]), (fwd_send.at[10 + a], fwd_got.at[10 + a])
        return (
            (c == 0, c == 1, remote(block, prev, *near, at(z, x, y, 1))),
            (c == 1, c == 0, remote(half, after, *near, at(z, x, y, 0))),
            (both(quarter == 3, not_last), both(quarter == 0, not_first), remote(block, prev, *far, at(z + 1, x, y, 0))),
            (both(quarter == 0, not_first), both(quarter == 3, not_last), remote(half, after, *far, at(z - 1, x, y, 1))),
        )

    def own_shared(a, target):
        arrived(target.at[pl.ds(BLOCK, BLOCK), :], got.at[8 + a])

    def relay(a, target):
        @pl.when(outer)
        def _():
            own_shared(a, target)
            for sends, _, copy in shared_copies(a, target)[2:]:
                pl.when(sends)(copy.start)

    def share(a, target):
        @pl.when(no(outer))
        def _():
            own_shared(a, target)

        for sends, _, copy in shared_copies(a, target)[:2]:
            pl.when(sends)(copy.start)

    def shared_in(a, target):
        @pl.when(quarter == 2)
        def _():
            arrived(target.at[pl.ds(0, BLOCK), :], halo_got.at[a])

        @pl.when(quarter == 1)
        def _():
            arrived(target.at[pl.ds(2 * BLOCK, HALF), :], halo_got.at[a])

        for sends, gets, copy in shared_copies(a, target):
            pl.when(sends)(copy.wait_send)
            pl.when(gets)(copy.wait_recv)

    def lay_out(keys, values, start, stop):
        def one(t, carry):
            row = pl.ds(pl.multiple_of(t * TILE, TILE), TILE)
            if keys is not None:
                kt[t] = keys[row, :]
            if values is not None:
                vt[t, 0:HD, :] = values[row, :].T
            return carry

        lax.fori_loop(start, stop, one, 0)

    def attend(queries, query_row, block, first_block, done_row, tiles):
        def scale(t, carry):
            row = pl.multiple_of(query_row + t * TILE, TILE)
            query = queries[pl.ds(row, TILE), :].astype(jnp.float32).T * LOG2_SCALE
            high = query.astype(jnp.bfloat16)
            qt[t, 0:HD, :] = high
            qt[t, HD:2 * HD, :] = (query - high.astype(jnp.float32)).astype(jnp.bfloat16)
            return carry

        first = first_block * 6

        def place(tile, m):
            return jnp.clip(lists[m, tile] - first, 0, tiles - 1)

        def scores(buffer, t, g):
            tile = block * FT + t
            top = None
            for j in range(G):
                key = kt[place(tile, g * G + j)]
                s = jnp.dot(jnp.concatenate([key, key], axis=1), qt[t], preferred_element_type=jnp.float32)
                buffer[j * TILE:(j + 1) * TILE, :] = s
                t_top = jnp.max(s, axis=0, keepdims=True)
                top = t_top if top is None else jnp.maximum(top, t_top)
            return top

        def weigh(buffer, t, g, peak):
            tile = block * FT + t
            total = None
            for j in range(G):
                m = g * G + j
                shift = peak + jnp.maximum(m + 1 - counts[tile], 0).astype(jnp.float32) * FAR
                w = jnp.exp2(buffer[j * TILE:(j + 1) * TILE, :] - shift).astype(jnp.bfloat16)
                part = jnp.dot(vt[place(tile, m)], w, preferred_element_type=jnp.float32)
                total = part if total is None else total + part
            return total

        def put(t):
            total = acc[...]
            row = pl.multiple_of(done_row + t * TILE, TILE)
            done[pl.ds(row, TILE), :] = (total[:HD] / total[HD:HD + 1]).T.astype(jnp.bfloat16)

        def query_tile(t, peak):
            acc[...] = jnp.zeros_like(acc)

            def step(i, peak):
                g = 2 * i
                top = scores(s1, t, g + 1)
                part = weigh(s0, t, g, peak)
                higher = jnp.maximum(peak, top)
                acc[...] = (acc[...] + part) * jnp.exp2(peak - higher)
                after = jnp.where(g + 2 < GROUPS, 0, 1)
                top = scores(s0, jnp.minimum(t + after, FT - 1), (g + 2) * (1 - after))
                part = weigh(s1, t, g + 1, higher)
                highest = jnp.where(after == 1, top, jnp.maximum(higher, top))
                acc[...] = (acc[...] + part) * jnp.where(after == 1, 1.0, jnp.exp2(higher - highest))
                return highest

            peak = lax.fori_loop(0, GROUPS // 2, step, peak)
            put(t)
            return peak

        def all_tiles():
            lax.fori_loop(0, FT, scale, 0)
            lax.fori_loop(0, FT, query_tile, scores(s0, 0, 0))

        def keep(t, carry):
            def step(g, peak):
                return jnp.maximum(peak, scores(kept.at[t * GROUPS + g], t, g))

            peaks[t] = lax.fori_loop(0, GROUPS, step, jnp.full((1, TILE), -FAR, jnp.float32))
            return carry

        def finish(t, carry):
            peak = peaks[t]
            acc[...] = jnp.zeros_like(acc)

            def step(i, carry):
                g = 2 * i
                part = weigh(kept.at[t * GROUPS + g], t, g, peak)
                acc[...] += part + weigh(kept.at[t * GROUPS + g + 1], t, g + 1, peak)
                return carry

            lax.fori_loop(0, GROUPS // 2, step, 0)
            put(t)
            return carry

        def first_stage():
            lax.fori_loop(0, FT, scale, 0)
            lax.fori_loop(0, FT, keep, 0)

        def second_stage():
            lax.fori_loop(0, FT, finish, 0)

        return all_tiles, first_stage, second_stage

    def give_back(done_row, head, half, core, local, s):
        for dh, dy in HALF_OFFSETS:
            px, py = (x // 2 * 2 + 2 * dh + half) % 4, (y + dy) % 4
            src = done.at[rows(done_row + ((px // 2) * 4 + py) * QROWS, QROWS), :]
            dst = out.at[:, columns(head)]

            def away():
                remote(src, dst, out_send.at[s], out_got, at(z, px, py, core)).start()

            if (dh, dy) != (0, 0):
                away()
            else:
                @pl.when(local)
                def _():
                    pltpu.make_async_copy(src, dst, out_got).start()

                @pl.when(no(local))
                def _():
                    away()

    def unit(queries, r, e):
        return attend(
            queries, e * HALF, 4 * z + 2 * c + e, 4 * z + 2 * c - 1, (2 * r + e) * HALF, PAIR // TILE
        )

    def return_unit(r, e):
        give_back((2 * r + e) * HALF, chip * 2 + r, c, e, both(mine, c == e), r)

    inner_e, outer_e = 1 - c, c
    near_tiles = (jnp.where(c == 0, 6, 0), jnp.where(c == 0, 21, 18))
    far_tiles = (jnp.where(c == 0, 0, 18), jnp.where(c == 0, 6, 21))
    send_q(0, qa)
    send_k(0, ka)
    send_v(0, va)
    vt[:, HD:VROWS, :] = jnp.ones((vt.shape[0], VROWS - HD, TILE), jnp.bfloat16)
    list_copy.wait()
    count_copy.wait()
    pass_on(0, ka)
    send_q(1, qb)
    pass_on(1, va)
    send_k(1, kb)
    send_v(1, vb)
    scatter_shared(q, ql, u * QROWS, QROWS, 8, q_got.at[2])
    scatter_shared(k, kl, BLOCK + u * KROWS, KROWS, 6, got.at[8])
    scatter_halo(k, kl, 0)
    arrived(qa, q_got.at[0])
    near_in(0, ka)
    near_in(1, va)
    lay_out(ka, va, *near_tiles)
    unit(qa, 0, inner_e)[0]()
    pass_on(2, kb)
    far_in(0, ka)
    far_in(1, va)
    lay_out(ka, va, *far_tiles)
    unit(qa, 0, outer_e)[0]()
    pass_on(3, vb)
    scatter_shared(v, vl, BLOCK + u * KROWS, KROWS, 7, got.at[9])
    scatter_halo(v, vl, 1)
    arrived(qb, q_got.at[1])
    near_in(2, kb)
    lay_out(kb, None, *near_tiles)
    _, first_stage, second_stage = unit(qb, 1, inner_e)
    first_stage()
    near_in(3, vb)
    lay_out(None, vb, *near_tiles)
    second_stage()
    relay(0, kl)
    share(0, kl)
    return_unit(1, inner_e)
    far_in(2, kb)
    far_in(3, vb)
    lay_out(kb, vb, *far_tiles)
    unit(qb, 1, outer_e)[0]()
    relay(1, vl)
    share(1, vl)
    return_unit(0, inner_e)
    return_unit(0, outer_e)
    return_unit(1, outer_e)
    arrived(ql, q_got.at[2])
    shared_in(0, kl)
    lay_out(kl, None, 0, ONE // TILE)
    _, first_stage, second_stage = attend(
        ql, 0, 4 * z + quarter, 4 * z + quarter - 1, 4 * HALF, ONE // TILE
    )
    first_stage()
    shared_in(1, vl)
    lay_out(None, vl, 0, ONE // TILE)
    second_stage()
    give_back(4 * HALF, MAIN + chip // 2, side, c, mine_l, 2)

    for i, target in enumerate((ka, va, kb, vb)):
        halos_sent(i, target)

    def sent(source, many, fewer, n, sem):
        for condition, size in ((fewer, n - 1), (no(fewer), n)):
            @pl.when(condition)
            def _():
                arrived(many(source, size), sem)

    def heads(source, n):
        return source.at[:, pl.ds(0, n * HD)]

    def parts(source, n):
        return source.at[pl.ds(0, n * QROWS), :]

    for a, source in enumerate((k, v, q)):
        sent(source, heads, mine, 16, send.at[a])
        sent(source, heads, mine, 16, send.at[3 + a])
        sent(source, heads, mine_l, 8, send.at[6 + a])
    for a, source in enumerate((k, v)):
        @pl.when(either(sends_prev, sends_next))
        def _():
            arrived(heads(source, 8), halo_send.at[a])
    sent(done, parts, mine, 16, out_send.at[0])
    sent(done, parts, mine, 16, out_send.at[1])
    sent(done, parts, mine_l, 8, out_send.at[2])
    arrived(out, out_got)


def per_device(queries, keys, values, tile_lists, tile_counts):
    anywhere = pl.BlockSpec(memory_space=pl.ANY)
    far = pl.BlockSpec(memory_space=pltpu.HBM)
    dma = pltpu.SemaphoreType.DMA

    def held(n):
        return pltpu.VMEM((n, HD), jnp.bfloat16)

    return pl.pallas_call(
        kernel,
        out_shape=jax.ShapeDtypeStruct((QROWS, HEADS * HD), jnp.bfloat16),
        in_specs=[far] * 5,
        out_specs=anywhere,
        scratch_shapes=[
            pltpu.SMEM(tile_lists.shape[::-1], jnp.int32), pltpu.SMEM(tile_counts.shape, jnp.int32), dma((2,)),
            held(2 * HALF), held(2 * HALF), held(HALF),
            held(PAIR), held(PAIR), held(ONE),
            held(PAIR), held(PAIR), held(ONE),
            held(5 * HALF),
            pltpu.VMEM((PAIR // TILE, TILE, HD), jnp.bfloat16),
            pltpu.VMEM((PAIR // TILE, VROWS, TILE), jnp.bfloat16),
            pltpu.VMEM((FT, 2 * HD, TILE), jnp.bfloat16),
            pltpu.VMEM((G * TILE, TILE), jnp.float32),
            pltpu.VMEM((G * TILE, TILE), jnp.float32),
            pltpu.VMEM((VROWS, TILE), jnp.float32),
            pltpu.VMEM((FT * GROUPS, G * TILE, TILE), jnp.float32),
            pltpu.VMEM((FT, 1, TILE), jnp.float32),
            dma((9,)), dma((10,)), dma((3,)), dma((12,)), dma((12,)), dma((2,)), dma((2,)), dma((3,)), dma,
        ],
        compiler_params=pltpu.CompilerParams(
            collective_id=0, has_side_effects=True, vmem_limit_bytes=52 * 1024 * 1024
        ),
        name="attention",
    )(tile_lists.T, tile_counts, queries, keys, values)


def solution(mesh):
    placed = (P(("blk", "uly"), None), P(("blk", "uly"), None), P(("blk", "uly"), None), P(), P())
    return jax.shard_map(
        per_device, mesh=mesh, in_specs=placed, out_specs=P(("blk", "uly"), None), check_vma=False
    )
```

```python
import functools

import jax
import jax.numpy as jnp
from jax import lax
from jax.experimental import pallas as pl
from jax.experimental.pallas import tpu as pltpu
from jax.sharding import PartitionSpec as P

HD = 128
TILE = 384
FT = 3
MAXT = 12
HEADS = 40
BLOCK = 2304
HALF = 1152
KROWS = 288
QROWS = 144
MAIN = 32
PAIR = 3 * BLOCK + HALF
ONE = 2 * BLOCK + HALF
VROWS = HD + 16
G = 3
GROUPS = MAXT // G
LOG2_SCALE = HD ** (-0.5) * 1.4426950408889634
FAR = 1e30
MESH = pl.DeviceIdType.MESH
OFFSETS = [(dx, (k - dx) % 4) for k in (1, 3, 2, 0) for dx in (1, 3, 2, 0)]
PAIR_OFFSETS = ((1, 0), (2, 1), (3, 0), (0, 1), (1, 1), (2, 0), (3, 1), (0, 0))
HALF_OFFSETS = ((0, 1), (1, 3), (1, 2), (0, 3), (1, 1), (0, 2), (1, 0), (0, 0))


def rows(start, size):
    return pl.ds(pl.multiple_of(start, 16), size)


def columns(head):
    return pl.ds(pl.multiple_of(head * HD, HD), HD)


def arrived(ref, sem):
    pltpu.make_async_copy(ref, ref, sem).wait()


def kernel(
    lists_in, counts_in, q, k, v, out,
    lists, counts, list_sem, qa, qb, ql, ka, kb, kl, va, vb, vl, done, kt, vt, qt, s0, s1, acc, kept, peaks,
    send, got, q_got, fwd_send, fwd_got, halo_send, halo_got, out_send, out_got,
):
    blk, u = lax.axis_index("blk"), lax.axis_index("uly")
    z, b, c = blk // 4, blk % 4, blk % 2
    xl = b // 2
    x, y = (u // 4) * 2 + xl, u % 4
    chip = x * 4 + y
    side = (y + z) % 2
    quarter = side * 2 + c
    outer = jnp.logical_or(quarter == 0, quarter == 3)
    not_first, not_last = z > 0, z < 3
    mine = xl == c
    mine_l = xl == side
    no = jnp.logical_not
    both = jnp.logical_and
    either = jnp.logical_or

    def at(z, x, y, c):
        return (z * 4 + (x % 2) * 2 + c, (x // 2) * 4 + y)

    def remote(src, dst, send_sem, recv_sem, device):
        return pltpu.make_async_remote_copy(
            src, dst, send_sem, recv_sem, device_id=device, device_id_type=MESH
        )

    list_copy = pltpu.make_async_copy(lists_in, lists, list_sem.at[0])
    count_copy = pltpu.make_async_copy(counts_in, counts, list_sem.at[1])
    list_copy.start()
    count_copy.start()

    barrier = pltpu.get_barrier_semaphore()

    def hello(device):
        pl.semaphore_signal(barrier, inc=1, device_id=device, device_id_type=MESH)

    for dx, dy in OFFSETS:
        there = ((x + dx) % 4, (y + dy) % 4)
        if (dx, dy) != (0, 0):
            hello(at(z, *there, c))
        hello(at(z, *there, 1 - c))
    up = either(c == 0, not_last)
    down = either(c == 1, not_first)

    @pl.when(both(c == 0, not_first))
    def _():
        hello(at(z - 1, x, y, 1))

    @pl.when(both(c == 1, not_last))
    def _():
        hello(at(z + 1, x, y, 0))

    pl.semaphore_wait(
        barrier,
        31 + jnp.where(both(c == 1, not_last), 1, 0) + jnp.where(both(c == 0, not_first), 1, 0),
    )

    e = b % 2

    def scatter(r, source, target, row, size, s, sem):
        for dx, dy in OFFSETS:
            px, py = (x + dx) % 4, (y + dy) % 4
            src = source.at[:, columns((px * 4 + py) * 2 + r)]
            dst = target.at[rows(row, size), :]

            def away():
                remote(src, dst, send.at[s], sem, at(z, px, py, xl)).start()

            if (dx, dy) != (0, 0):
                away()
            else:
                @pl.when(mine)
                def _():
                    pltpu.make_async_copy(src, dst, sem).start()

                @pl.when(no(mine))
                def _():
                    away()

    def scatter_shared(source, target, row, size, s, sem):
        for dx, dp in PAIR_OFFSETS:
            px, pp = (x + dx) % 4, (y // 2 + dp) % 2
            src = source.at[:, columns(MAIN + px * 2 + pp)]
            dst = target.at[rows(row, size), :]

            def away():
                remote(src, dst, send.at[s], sem, at(z, px, pp * 2 + (xl + z) % 2, e)).start()

            if (dx, dp) != (0, 0):
                away()
            else:
                @pl.when(mine_l)
                def _():
                    pltpu.make_async_copy(src, dst, sem).start()

                @pl.when(no(mine_l))
                def _():
                    away()

    sends_prev, sends_next = b == 1, both(b == 2, u < 4)

    def scatter_halo(source, target, a):
        @pl.when(sends_prev)
        def _():
            for dx, dp in PAIR_OFFSETS:
                px, pp = (x + dx) % 4, (y // 2 + dp) % 2
                remote(
                    source.at[:, columns(MAIN + px * 2 + pp)], target.at[rows(u * KROWS, KROWS), :],
                    halo_send.at[a], halo_got.at[a], at(z, px, pp * 2 + (1 + z) % 2, 0),
                ).start()

        @pl.when(sends_next)
        def _():
            for dx, dp in PAIR_OFFSETS:
                px, pp = (x + dx) % 4, (y // 2 + dp) % 2
                remote(
                    source.at[:, columns(MAIN + px * 2 + pp)],
                    target.at[rows(2 * BLOCK + (u % 4) * KROWS, KROWS), :],
                    halo_send.at[a], halo_got.at[a], at(z, px, pp * 2 + z % 2, 1),
                ).start()

    kv_row, q_row = BLOCK * (1 + e) + u * KROWS, HALF * e + u * QROWS

    def send_k(r, target):
        scatter(r, k, target, kv_row, KROWS, 3 * r, got.at[4 * r + e])

    def send_v(r, target):
        scatter(r, v, target, kv_row, KROWS, 3 * r + 1, got.at[4 * r + 2 + e])

    def send_q(r, target):
        scatter(r, q, target, q_row, QROWS, 3 * r + 2, q_got.at[r])

    def halos(i, target):
        return (
            remote(
                target.at[pl.ds(2 * BLOCK, BLOCK), :], target.at[pl.ds(0, BLOCK), :],
                fwd_send.at[2 * i], fwd_got.at[2 * i], at(z + c, x, y, 1 - c),
            ),
            remote(
                target.at[pl.ds(BLOCK, HALF), :], target.at[pl.ds(3 * BLOCK, HALF), :],
                fwd_send.at[2 * i + 1], fwd_got.at[2 * i + 1], at(z - 1 + c, x, y, 1 - c),
            ),
        )

    def pass_on(i, target):
        to_up, to_down = halos(i, target)
        arrived(target.at[pl.ds(2 * BLOCK, BLOCK), :], got.at[2 * i + 1])
        arrived(target.at[pl.ds(BLOCK, BLOCK), :], got.at[2 * i])
        pl.when(c == 0)(to_up.start)
        pl.when(c == 1)(to_down.start)
        pl.when(both(c == 1, not_last))(to_up.start)
        pl.when(both(c == 0, not_first))(to_down.start)

    def near_in(i, target):
        to_up, to_down = halos(i, target)
        pl.when(c == 1)(to_up.wait_recv)
        pl.when(c == 0)(to_down.wait_recv)

    def far_in(i, target):
        to_up, to_down = halos(i, target)
        pl.when(both(c == 0, not_first))(to_up.wait_recv)
        pl.when(both(c == 1, not_last))(to_down.wait_recv)

    def halos_sent(i, target):
        to_up, to_down = halos(i, target)

        @pl.when(up)
        def _():
            to_up.wait_send()

        @pl.when(down)
        def _():
            to_down.wait_send()

    def shared_copies(a, target):
        block, half = target.at[pl.ds(BLOCK, BLOCK), :], target.at[pl.ds(BLOCK, HALF), :]
        prev, after = target.at[pl.ds(0, BLOCK), :], target.at[pl.ds(2 * BLOCK, HALF), :]
        near, far = (fwd_send.at[8 + a], fwd_got.at[8 + a]), (fwd_send.at[10 + a], fwd_got.at[10 + a])
        return (
            (c == 0, c == 1, remote(block, prev, *near, at(z, x, y, 1))),
            (c == 1, c == 0, remote(half, after, *near, at(z, x, y, 0))),
            (both(quarter == 3, not_last), both(quarter == 0, not_first), remote(block, prev, *far, at(z + 1, x, y, 0))),
            (both(quarter == 0, not_first), both(quarter == 3, not_last), remote(half, after, *far, at(z - 1, x, y, 1))),
        )

    def own_shared(a, target):
        arrived(target.at[pl.ds(BLOCK, BLOCK), :], got.at[8 + a])

    def relay(a, target):
        @pl.when(outer)
        def _():
            own_shared(a, target)
            for sends, _, copy in shared_copies(a, target)[2:]:
                pl.when(sends)(copy.start)

    def share(a, target):
        @pl.when(no(outer))
        def _():
            own_shared(a, target)

        for sends, _, copy in shared_copies(a, target)[:2]:
            pl.when(sends)(copy.start)

    def shared_in(a, target):
        @pl.when(quarter == 2)
        def _():
            arrived(target.at[pl.ds(0, BLOCK), :], halo_got.at[a])

        @pl.when(quarter == 1)
        def _():
            arrived(target.at[pl.ds(2 * BLOCK, HALF), :], halo_got.at[a])

        for sends, gets, copy in shared_copies(a, target):
            pl.when(sends)(copy.wait_send)
            pl.when(gets)(copy.wait_recv)

    def lay_out(keys, values, start, stop):
        def one(t, carry):
            row = pl.ds(pl.multiple_of(t * TILE, TILE), TILE)
            if keys is not None:
                kt[t] = keys[row, :]
            if values is not None:
                vt[t, 0:HD, :] = values[row, :].T
            return carry

        lax.fori_loop(start, stop, one, 0)

    def attend(queries, query_row, block, first_block, done_row, tiles):
        def scale(t, carry):
            row = pl.multiple_of(query_row + t * TILE, TILE)
            query = queries[pl.ds(row, TILE), :].astype(jnp.float32).T * LOG2_SCALE
            high = query.astype(jnp.bfloat16)
            qt[t, 0:HD, :] = high
            qt[t, HD:2 * HD, :] = (query - high.astype(jnp.float32)).astype(jnp.bfloat16)
            return carry

        first = first_block * 6

        def place(tile, m):
            return jnp.clip(lists[m, tile] - first, 0, tiles - 1)

        def scores(buffer, t, g):
            tile = block * FT + t
            top = None
            for j in range(G):
                key = kt[place(tile, g * G + j)]
                s = jnp.dot(jnp.concatenate([key, key], axis=1), qt[t], preferred_element_type=jnp.float32)
                buffer[j * TILE:(j + 1) * TILE, :] = s
                t_top = jnp.max(s, axis=0, keepdims=True)
                top = t_top if top is None else jnp.maximum(top, t_top)
            return top

        def weigh(buffer, t, g, peak):
            tile = block * FT + t
            total = None
            for j in range(G):
                m = g * G + j
                shift = peak + jnp.maximum(m + 1 - counts[tile], 0).astype(jnp.float32) * FAR
                w = jnp.exp2(buffer[j * TILE:(j + 1) * TILE, :] - shift).astype(jnp.bfloat16)
                part = jnp.dot(vt[place(tile, m)], w, preferred_element_type=jnp.float32)
                total = part if total is None else total + part
            return total

        def put(t):
            total = acc[...]
            row = pl.multiple_of(done_row + t * TILE, TILE)
            done[pl.ds(row, TILE), :] = (total[:HD] / total[HD:HD + 1]).T.astype(jnp.bfloat16)

        def query_tile(t, peak):
            acc[...] = jnp.zeros_like(acc)

            def step(i, peak):
                g = 2 * i
                top = scores(s1, t, g + 1)
                part = weigh(s0, t, g, peak)
                higher = jnp.maximum(peak, top)
                acc[...] = (acc[...] + part) * jnp.exp2(peak - higher)
                after = jnp.where(g + 2 < GROUPS, 0, 1)
                top = scores(s0, jnp.minimum(t + after, FT - 1), (g + 2) * (1 - after))
                part = weigh(s1, t, g + 1, higher)
                highest = jnp.where(after == 1, top, jnp.maximum(higher, top))
                acc[...] = (acc[...] + part) * jnp.where(after == 1, 1.0, jnp.exp2(higher - highest))
                return highest

            peak = lax.fori_loop(0, GROUPS // 2, step, peak)
            put(t)
            return peak

        def all_tiles():
            lax.fori_loop(0, FT, scale, 0)
            lax.fori_loop(0, FT, query_tile, scores(s0, 0, 0))

        def keep(t, carry):
            def step(g, peak):
                return jnp.maximum(peak, scores(kept.at[t * GROUPS + g], t, g))

            peaks[t] = lax.fori_loop(0, GROUPS, step, jnp.full((1, TILE), -FAR, jnp.float32))
            return carry

        def finish(t, carry):
            peak = peaks[t]
            acc[...] = jnp.zeros_like(acc)

            def step(i, carry):
                g = 2 * i
                part = weigh(kept.at[t * GROUPS + g], t, g, peak)
                acc[...] += part + weigh(kept.at[t * GROUPS + g + 1], t, g + 1, peak)
                return carry

            lax.fori_loop(0, GROUPS // 2, step, 0)
            put(t)
            return carry

        def first_stage():
            lax.fori_loop(0, FT, scale, 0)
            lax.fori_loop(0, FT, keep, 0)

        def second_stage():
            lax.fori_loop(0, FT, finish, 0)

        return all_tiles, first_stage, second_stage

    def give_back(done_row, head, half, core, local, s):
        for dh, dy in HALF_OFFSETS:
            px, py = (x // 2 * 2 + 2 * dh + half) % 4, (y + dy) % 4
            src = done.at[rows(done_row + ((px // 2) * 4 + py) * QROWS, QROWS), :]
            dst = out.at[:, columns(head)]

            def away():
                remote(src, dst, out_send.at[s], out_got, at(z, px, py, core)).start()

            if (dh, dy) != (0, 0):
                away()
            else:
                @pl.when(local)
                def _():
                    pltpu.make_async_copy(src, dst, out_got).start()

                @pl.when(no(local))
                def _():
                    away()

    def unit(queries, r, e):
        return attend(
            queries, e * HALF, 4 * z + 2 * c + e, 4 * z + 2 * c - 1, (2 * r + e) * HALF, PAIR // TILE
        )

    def return_unit(r, e):
        give_back((2 * r + e) * HALF, chip * 2 + r, c, e, both(mine, c == e), r)

    inner_e, outer_e = 1 - c, c
    near_tiles = (jnp.where(c == 0, 6, 0), jnp.where(c == 0, 21, 18))
    far_tiles = (jnp.where(c == 0, 0, 18), jnp.where(c == 0, 6, 21))
    send_q(0, qa)
    send_k(0, ka)
    send_v(0, va)
    vt[:, HD:VROWS, :] = jnp.ones((vt.shape[0], VROWS - HD, TILE), jnp.bfloat16)
    list_copy.wait()
    count_copy.wait()
    pass_on(0, ka)
    send_q(1, qb)
    pass_on(1, va)
    send_k(1, kb)
    send_v(1, vb)
    scatter_shared(q, ql, u * QROWS, QROWS, 8, q_got.at[2])
    scatter_shared(k, kl, BLOCK + u * KROWS, KROWS, 6, got.at[8])
    scatter_halo(k, kl, 0)
    arrived(qa, q_got.at[0])
    near_in(0, ka)
    near_in(1, va)
    lay_out(ka, va, *near_tiles)
    unit(qa, 0, inner_e)[0]()
    pass_on(2, kb)
    far_in(0, ka)
    far_in(1, va)
    lay_out(ka, va, *far_tiles)
    unit(qa, 0, outer_e)[0]()
    pass_on(3, vb)
    scatter_shared(v, vl, BLOCK + u * KROWS, KROWS, 7, got.at[9])
    scatter_halo(v, vl, 1)
    arrived(qb, q_got.at[1])
    near_in(2, kb)
    lay_out(kb, None, *near_tiles)
    _, first_stage, second_stage = unit(qb, 1, inner_e)
    first_stage()
    near_in(3, vb)
    lay_out(None, vb, *near_tiles)
    second_stage()
    relay(0, kl)
    share(0, kl)
    return_unit(1, inner_e)
    far_in(2, kb)
    far_in(3, vb)
    lay_out(kb, vb, *far_tiles)
    unit(qb, 1, outer_e)[0]()
    relay(1, vl)
    share(1, vl)
    return_unit(0, inner_e)
    return_unit(0, outer_e)
    return_unit(1, outer_e)
    arrived(ql, q_got.at[2])
    shared_in(0, kl)
    lay_out(kl, None, 0, ONE // TILE)
    _, first_stage, second_stage = attend(
        ql, 0, 4 * z + quarter, 4 * z + quarter - 1, 4 * HALF, ONE // TILE
    )
    first_stage()
    shared_in(1, vl)
    lay_out(None, vl, 0, ONE // TILE)
    second_stage()
    give_back(4 * HALF, MAIN + chip // 2, side, c, mine_l, 2)

    for i, target in enumerate((ka, va, kb, vb)):
        halos_sent(i, target)

    def sent(source, many, fewer, n, sem):
        for condition, size in ((fewer, n - 1), (no(fewer), n)):
            @pl.when(condition)
            def _():
                arrived(many(source, size), sem)

    def heads(source, n):
        return source.at[:, pl.ds(0, n * HD)]

    def parts(source, n):
        return source.at[pl.ds(0, n * QROWS), :]

    for a, source in enumerate((k, v, q)):
        sent(source, heads, mine, 16, send.at[a])
        sent(source, heads, mine, 16, send.at[3 + a])
        sent(source, heads, mine_l, 8, send.at[6 + a])
    for a, source in enumerate((k, v)):
        @pl.when(either(sends_prev, sends_next))
        def _():
            arrived(heads(source, 8), halo_send.at[a])
    sent(done, parts, mine, 16, out_send.at[0])
    sent(done, parts, mine, 16, out_send.at[1])
    sent(done, parts, mine_l, 8, out_send.at[2])
    arrived(out, out_got)


def per_device(queries, keys, values, tile_lists, tile_counts):
    anywhere = pl.BlockSpec(memory_space=pl.ANY)
    far = pl.BlockSpec(memory_space=pltpu.HBM)
    dma = pltpu.SemaphoreType.DMA

    def held(n):
        return pltpu.VMEM((n, HD), jnp.bfloat16)

    return pl.pallas_call(
        kernel,
        out_shape=jax.ShapeDtypeStruct((QROWS, HEADS * HD), jnp.bfloat16),
        in_specs=[far] * 5,
        out_specs=anywhere,
        scratch_shapes=[
            pltpu.SMEM(tile_lists.shape[::-1], jnp.int32), pltpu.SMEM(tile_counts.shape, jnp.int32), dma((2,)),
            held(2 * HALF), held(2 * HALF), held(HALF),
            held(PAIR), held(PAIR), held(ONE),
            held(PAIR), held(PAIR), held(ONE),
            held(5 * HALF),
            pltpu.VMEM((PAIR // TILE, TILE, HD), jnp.bfloat16),
            pltpu.VMEM((PAIR // TILE, VROWS, TILE), jnp.bfloat16),
            pltpu.VMEM((FT, 2 * HD, TILE), jnp.bfloat16),
            pltpu.VMEM((G * TILE, TILE), jnp.float32),
            pltpu.VMEM((G * TILE, TILE), jnp.float32),
            pltpu.VMEM((VROWS, TILE), jnp.float32),
            pltpu.VMEM((FT * GROUPS, G * TILE, TILE), jnp.float32),
            pltpu.VMEM((FT, 1, TILE), jnp.float32),
            dma((9,)), dma((10,)), dma((3,)), dma((12,)), dma((12,)), dma((2,)), dma((2,)), dma((3,)), dma,
        ],
        compiler_params=pltpu.CompilerParams(
            collective_id=0, has_side_effects=True, vmem_limit_bytes=52 * 1024 * 1024
        ),
        name="attention",
    )(tile_lists.T, tile_counts, queries, keys, values)


def solution(mesh):
    placed = (P(("blk", "uly"), None), P(("blk", "uly"), None), P(("blk", "uly"), None), P(), P())
    return jax.shard_map(
        per_device, mesh=mesh, in_specs=placed, out_specs=P(("blk", "uly"), None), check_vma=False
    )
```

```python
import functools

import jax
import jax.numpy as jnp
from jax import lax
from jax.experimental import pallas as pl
from jax.experimental.pallas import tpu as pltpu
from jax.sharding import PartitionSpec as P

HD = 128
TILE = 384
FT = 3
MAXT = 12
HEADS = 40
BLOCK = 2304
HALF = 1152
KROWS = 288
QROWS = 144
MAIN = 32
PAIR = 3 * BLOCK + HALF
ONE = 2 * BLOCK + HALF
VROWS = HD + 16
G = 6
GROUPS = MAXT // G
LOG2_SCALE = HD ** (-0.5) * 1.4426950408889634
FAR = 1e30
MESH = pl.DeviceIdType.MESH
OFFSETS = [(dx, (k - dx) % 4) for k in (1, 3, 2, 0) for dx in (1, 3, 2, 0)]
PAIR_OFFSETS = ((1, 0), (2, 1), (3, 0), (0, 1), (1, 1), (2, 0), (3, 1), (0, 0))
HALF_OFFSETS = ((0, 1), (1, 3), (1, 2), (0, 3), (1, 1), (0, 2), (1, 0), (0, 0))


def rows(start, size):
    return pl.ds(pl.multiple_of(start, 16), size)


def columns(head):
    return pl.ds(pl.multiple_of(head * HD, HD), HD)


def arrived(ref, sem):
    pltpu.make_async_copy(ref, ref, sem).wait()


def kernel(
    lists_in, counts_in, q, k, v, out,
    lists, counts, list_sem, qa, qb, ql, ka, kb, kl, va, vb, vl, done, kt, vt, qt, s0, s1, acc, kept, peaks,
    send, got, q_got, fwd_send, fwd_got, halo_send, halo_got, out_send, out_got,
):
    blk, u = lax.axis_index("blk"), lax.axis_index("uly")
    z, b, c = blk // 4, blk % 4, blk % 2
    xl = b // 2
    x, y = (u // 4) * 2 + xl, u % 4
    chip = x * 4 + y
    side = (y + z) % 2
    quarter = side * 2 + c
    outer = jnp.logical_or(quarter == 0, quarter == 3)
    not_first, not_last = z > 0, z < 3
    mine = xl == c
    mine_l = xl == side
    no = jnp.logical_not
    both = jnp.logical_and
    either = jnp.logical_or

    def at(z, x, y, c):
        return (z * 4 + (x % 2) * 2 + c, (x // 2) * 4 + y)

    def remote(src, dst, send_sem, recv_sem, device):
        return pltpu.make_async_remote_copy(
            src, dst, send_sem, recv_sem, device_id=device, device_id_type=MESH
        )

    list_copy = pltpu.make_async_copy(lists_in, lists, list_sem.at[0])
    count_copy = pltpu.make_async_copy(counts_in, counts, list_sem.at[1])
    list_copy.start()
    count_copy.start()

    barrier = pltpu.get_barrier_semaphore()

    def hello(device):
        pl.semaphore_signal(barrier, inc=1, device_id=device, device_id_type=MESH)

    for dx, dy in OFFSETS:
        there = ((x + dx) % 4, (y + dy) % 4)
        if (dx, dy) != (0, 0):
            hello(at(z, *there, c))
        hello(at(z, *there, 1 - c))
    up = either(c == 0, not_last)
    down = either(c == 1, not_first)

    @pl.when(both(c == 0, not_first))
    def _():
        hello(at(z - 1, x, y, 1))

    @pl.when(both(c == 1, not_last))
    def _():
        hello(at(z + 1, x, y, 0))

    pl.semaphore_wait(
        barrier,
        31 + jnp.where(both(c == 1, not_last), 1, 0) + jnp.where(both(c == 0, not_first), 1, 0),
    )

    e = b % 2

    def scatter(r, source, target, row, size, s, sem):
        for dx, dy in OFFSETS:
            px, py = (x + dx) % 4, (y + dy) % 4
            src = source.at[:, columns((px * 4 + py) * 2 + r)]
            dst = target.at[rows(row, size), :]

            def away():
                remote(src, dst, send.at[s], sem, at(z, px, py, xl)).start()

            if (dx, dy) != (0, 0):
                away()
            else:
                @pl.when(mine)
                def _():
                    pltpu.make_async_copy(src, dst, sem).start()

                @pl.when(no(mine))
                def _():
                    away()

    def scatter_shared(source, target, row, size, s, sem):
        for dx, dp in PAIR_OFFSETS:
            px, pp = (x + dx) % 4, (y // 2 + dp) % 2
            src = source.at[:, columns(MAIN + px * 2 + pp)]
            dst = target.at[rows(row, size), :]

            def away():
                remote(src, dst, send.at[s], sem, at(z, px, pp * 2 + (xl + z) % 2, e)).start()

            if (dx, dp) != (0, 0):
                away()
            else:
                @pl.when(mine_l)
                def _():
                    pltpu.make_async_copy(src, dst, sem).start()

                @pl.when(no(mine_l))
                def _():
                    away()

    sends_prev, sends_next = b == 1, both(b == 2, u < 4)

    def scatter_halo(source, target, a):
        @pl.when(sends_prev)
        def _():
            for dx, dp in PAIR_OFFSETS:
                px, pp = (x + dx) % 4, (y // 2 + dp) % 2
                remote(
                    source.at[:, columns(MAIN + px * 2 + pp)], target.at[rows(u * KROWS, KROWS), :],
                    halo_send.at[a], halo_got.at[a], at(z, px, pp * 2 + (1 + z) % 2, 0),
                ).start()

        @pl.when(sends_next)
        def _():
            for dx, dp in PAIR_OFFSETS:
                px, pp = (x + dx) % 4, (y // 2 + dp) % 2
                remote(
                    source.at[:, columns(MAIN + px * 2 + pp)],
                    target.at[rows(2 * BLOCK + (u % 4) * KROWS, KROWS), :],
                    halo_send.at[a], halo_got.at[a], at(z, px, pp * 2 + z % 2, 1),
                ).start()

    kv_row, q_row = BLOCK * (1 + e) + u * KROWS, HALF * e + u * QROWS

    def send_k(r, target):
        scatter(r, k, target, kv_row, KROWS, 3 * r, got.at[4 * r + e])

    def send_v(r, target):
        scatter(r, v, target, kv_row, KROWS, 3 * r + 1, got.at[4 * r + 2 + e])

    def send_q(r, target):
        scatter(r, q, target, q_row, QROWS, 3 * r + 2, q_got.at[r])

    def halos(i, target):
        return (
            remote(
                target.at[pl.ds(2 * BLOCK, BLOCK), :], target.at[pl.ds(0, BLOCK), :],
                fwd_send.at[2 * i], fwd_got.at[2 * i], at(z + c, x, y, 1 - c),
            ),
            remote(
                target.at[pl.ds(BLOCK, HALF), :], target.at[pl.ds(3 * BLOCK, HALF), :],
                fwd_send.at[2 * i + 1], fwd_got.at[2 * i + 1], at(z - 1 + c, x, y, 1 - c),
            ),
        )

    def pass_on(i, target):
        to_up, to_down = halos(i, target)
        arrived(target.at[pl.ds(2 * BLOCK, BLOCK), :], got.at[2 * i + 1])
        arrived(target.at[pl.ds(BLOCK, BLOCK), :], got.at[2 * i])
        pl.when(c == 0)(to_up.start)
        pl.when(c == 1)(to_down.start)
        pl.when(both(c == 1, not_last))(to_up.start)
        pl.when(both(c == 0, not_first))(to_down.start)

    def near_in(i, target):
        to_up, to_down = halos(i, target)
        pl.when(c == 1)(to_up.wait_recv)
        pl.when(c == 0)(to_down.wait_recv)

    def far_in(i, target):
        to_up, to_down = halos(i, target)
        pl.when(both(c == 0, not_first))(to_up.wait_recv)
        pl.when(both(c == 1, not_last))(to_down.wait_recv)

    def halos_sent(i, target):
        to_up, to_down = halos(i, target)

        @pl.when(up)
        def _():
            to_up.wait_send()

        @pl.when(down)
        def _():
            to_down.wait_send()

    def shared_copies(a, target):
        block, half = target.at[pl.ds(BLOCK, BLOCK), :], target.at[pl.ds(BLOCK, HALF), :]
        prev, after = target.at[pl.ds(0, BLOCK), :], target.at[pl.ds(2 * BLOCK, HALF), :]
        near, far = (fwd_send.at[8 + a], fwd_got.at[8 + a]), (fwd_send.at[10 + a], fwd_got.at[10 + a])
        return (
            (c == 0, c == 1, remote(block, prev, *near, at(z, x, y, 1))),
            (c == 1, c == 0, remote(half, after, *near, at(z, x, y, 0))),
            (both(quarter == 3, not_last), both(quarter == 0, not_first), remote(block, prev, *far, at(z + 1, x, y, 0))),
            (both(quarter == 0, not_first), both(quarter == 3, not_last), remote(half, after, *far, at(z - 1, x, y, 1))),
        )

    def own_shared(a, target):
        arrived(target.at[pl.ds(BLOCK, BLOCK), :], got.at[8 + a])

    def relay(a, target):
        @pl.when(outer)
        def _():
            own_shared(a, target)
            for sends, _, copy in shared_copies(a, target)[2:]:
                pl.when(sends)(copy.start)

    def share(a, target):
        @pl.when(no(outer))
        def _():
            own_shared(a, target)

        for sends, _, copy in shared_copies(a, target)[:2]:
            pl.when(sends)(copy.start)

    def shared_in(a, target):
        @pl.when(quarter == 2)
        def _():
            arrived(target.at[pl.ds(0, BLOCK), :], halo_got.at[a])

        @pl.when(quarter == 1)
        def _():
            arrived(target.at[pl.ds(2 * BLOCK, HALF), :], halo_got.at[a])

        for sends, gets, copy in shared_copies(a, target):
            pl.when(sends)(copy.wait_send)
            pl.when(gets)(copy.wait_recv)

    def lay_out(keys, values, start, stop):
        def one(t, carry):
            row = pl.ds(pl.multiple_of(t * TILE, TILE), TILE)
            if keys is not None:
                kt[t] = keys[row, :]
            if values is not None:
                vt[t, 0:HD, :] = values[row, :].T
            return carry

        lax.fori_loop(start, stop, one, 0)

    def attend(queries, query_row, block, first_block, done_row, tiles):
        def scale(t, carry):
            row = pl.multiple_of(query_row + t * TILE, TILE)
            query = queries[pl.ds(row, TILE), :].astype(jnp.float32).T * LOG2_SCALE
            high = query.astype(jnp.bfloat16)
            qt[t, 0:HD, :] = high
            qt[t, HD:2 * HD, :] = (query - high.astype(jnp.float32)).astype(jnp.bfloat16)
            return carry

        first = first_block * 6

        def place(tile, m):
            return jnp.clip(lists[m, tile] - first, 0, tiles - 1)

        def scores(buffer, t, g):
            tile = block * FT + t
            top = None
            for j in range(G):
                key = kt[place(tile, g * G + j)]
                s = jnp.dot(jnp.concatenate([key, key], axis=1), qt[t], preferred_element_type=jnp.float32)
                buffer[j * TILE:(j + 1) * TILE, :] = s
                t_top = jnp.max(s, axis=0, keepdims=True)
                top = t_top if top is None else jnp.maximum(top, t_top)
            return top

        def weigh(buffer, t, g, peak):
            tile = block * FT + t
            total = None
            for j in range(G):
                m = g * G + j
                shift = peak + jnp.maximum(m + 1 - counts[tile], 0).astype(jnp.float32) * FAR
                w = jnp.exp2(buffer[j * TILE:(j + 1) * TILE, :] - shift).astype(jnp.bfloat16)
                part = jnp.dot(vt[place(tile, m)], w, preferred_element_type=jnp.float32)
                total = part if total is None else total + part
            return total

        def put(t):
            total = acc[...]
            row = pl.multiple_of(done_row + t * TILE, TILE)
            done[pl.ds(row, TILE), :] = (total[:HD] / total[HD:HD + 1]).T.astype(jnp.bfloat16)

        def query_tile(t, peak):
            acc[...] = jnp.zeros_like(acc)

            def step(i, peak):
                g = 2 * i
                top = scores(s1, t, g + 1)
                part = weigh(s0, t, g, peak)
                higher = jnp.maximum(peak, top)
                acc[...] = (acc[...] + part) * jnp.exp2(peak - higher)
                after = jnp.where(g + 2 < GROUPS, 0, 1)
                top = scores(s0, jnp.minimum(t + after, FT - 1), (g + 2) * (1 - after))
                part = weigh(s1, t, g + 1, higher)
                highest = jnp.where(after == 1, top, jnp.maximum(higher, top))
                acc[...] = (acc[...] + part) * jnp.where(after == 1, 1.0, jnp.exp2(higher - highest))
                return highest

            peak = lax.fori_loop(0, GROUPS // 2, step, peak)
            put(t)
            return peak

        def all_tiles():
            lax.fori_loop(0, FT, scale, 0)
            lax.fori_loop(0, FT, query_tile, scores(s0, 0, 0))

        def keep(t, carry):
            def step(g, peak):
                return jnp.maximum(peak, scores(kept.at[t * GROUPS + g], t, g))

            peaks[t] = lax.fori_loop(0, GROUPS, step, jnp.full((1, TILE), -FAR, jnp.float32))
            return carry

        def finish(t, carry):
            peak = peaks[t]
            acc[...] = jnp.zeros_like(acc)

            def step(i, carry):
                g = 2 * i
                part = weigh(kept.at[t * GROUPS + g], t, g, peak)
                acc[...] += part + weigh(kept.at[t * GROUPS + g + 1], t, g + 1, peak)
                return carry

            lax.fori_loop(0, GROUPS // 2, step, 0)
            put(t)
            return carry

        def first_stage():
            lax.fori_loop(0, FT, scale, 0)
            lax.fori_loop(0, FT, keep, 0)

        def second_stage():
            lax.fori_loop(0, FT, finish, 0)

        return all_tiles, first_stage, second_stage

    def give_back(done_row, head, half, core, local, s):
        for dh, dy in HALF_OFFSETS:
            px, py = (x // 2 * 2 + 2 * dh + half) % 4, (y + dy) % 4
            src = done.at[rows(done_row + ((px // 2) * 4 + py) * QROWS, QROWS), :]
            dst = out.at[:, columns(head)]

            def away():
                remote(src, dst, out_send.at[s], out_got, at(z, px, py, core)).start()

            if (dh, dy) != (0, 0):
                away()
            else:
                @pl.when(local)
                def _():
                    pltpu.make_async_copy(src, dst, out_got).start()

                @pl.when(no(local))
                def _():
                    away()

    def unit(queries, r, e):
        return attend(
            queries, e * HALF, 4 * z + 2 * c + e, 4 * z + 2 * c - 1, (2 * r + e) * HALF, PAIR // TILE
        )

    def return_unit(r, e):
        give_back((2 * r + e) * HALF, chip * 2 + r, c, e, both(mine, c == e), r)

    inner_e, outer_e = 1 - c, c
    near_tiles = (jnp.where(c == 0, 6, 0), jnp.where(c == 0, 21, 18))
    far_tiles = (jnp.where(c == 0, 0, 18), jnp.where(c == 0, 6, 21))
    send_q(0, qa)
    send_k(0, ka)
    send_v(0, va)
    vt[:, HD:VROWS, :] = jnp.ones((vt.shape[0], VROWS - HD, TILE), jnp.bfloat16)
    list_copy.wait()
    count_copy.wait()
    pass_on(0, ka)
    send_q(1, qb)
    pass_on(1, va)
    send_k(1, kb)
    send_v(1, vb)
    scatter_shared(q, ql, u * QROWS, QROWS, 8, q_got.at[2])
    scatter_shared(k, kl, BLOCK + u * KROWS, KROWS, 6, got.at[8])
    scatter_halo(k, kl, 0)
    arrived(qa, q_got.at[0])
    near_in(0, ka)
    near_in(1, va)
    lay_out(ka, va, *near_tiles)
    unit(qa, 0, inner_e)[0]()
    pass_on(2, kb)
    far_in(0, ka)
    far_in(1, va)
    lay_out(ka, va, *far_tiles)
    unit(qa, 0, outer_e)[0]()
    pass_on(3, vb)
    scatter_shared(v, vl, BLOCK + u * KROWS, KROWS, 7, got.at[9])
    scatter_halo(v, vl, 1)
    arrived(qb, q_got.at[1])
    near_in(2, kb)
    lay_out(kb, None, *near_tiles)
    _, first_stage, second_stage = unit(qb, 1, inner_e)
    first_stage()
    near_in(3, vb)
    lay_out(None, vb, *near_tiles)
    second_stage()
    relay(0, kl)
    share(0, kl)
    far_in(2, kb)
    far_in(3, vb)
    lay_out(kb, vb, *far_tiles)
    unit(qb, 1, outer_e)[0]()
    relay(1, vl)
    share(1, vl)
    return_unit(0, inner_e)
    return_unit(0, outer_e)
    return_unit(1, inner_e)
    return_unit(1, outer_e)
    arrived(ql, q_got.at[2])
    shared_in(0, kl)
    lay_out(kl, None, 0, ONE // TILE)
    _, first_stage, second_stage = attend(
        ql, 0, 4 * z + quarter, 4 * z + quarter - 1, 4 * HALF, ONE // TILE
    )
    first_stage()
    shared_in(1, vl)
    lay_out(None, vl, 0, ONE // TILE)
    second_stage()
    give_back(4 * HALF, MAIN + chip // 2, side, c, mine_l, 2)

    for i, target in enumerate((ka, va, kb, vb)):
        halos_sent(i, target)

    def sent(source, many, fewer, n, sem):
        for condition, size in ((fewer, n - 1), (no(fewer), n)):
            @pl.when(condition)
            def _():
                arrived(many(source, size), sem)

    def heads(source, n):
        return source.at[:, pl.ds(0, n * HD)]

    def parts(source, n):
        return source.at[pl.ds(0, n * QROWS), :]

    for a, source in enumerate((k, v, q)):
        sent(source, heads, mine, 16, send.at[a])
        sent(source, heads, mine, 16, send.at[3 + a])
        sent(source, heads, mine_l, 8, send.at[6 + a])
    for a, source in enumerate((k, v)):
        @pl.when(either(sends_prev, sends_next))
        def _():
            arrived(heads(source, 8), halo_send.at[a])
    sent(done, parts, mine, 16, out_send.at[0])
    sent(done, parts, mine, 16, out_send.at[1])
    sent(done, parts, mine_l, 8, out_send.at[2])
    arrived(out, out_got)


def per_device(queries, keys, values, tile_lists, tile_counts):
    anywhere = pl.BlockSpec(memory_space=pl.ANY)
    far = pl.BlockSpec(memory_space=pltpu.HBM)
    dma = pltpu.SemaphoreType.DMA

    def held(n):
        return pltpu.VMEM((n, HD), jnp.bfloat16)

    return pl.pallas_call(
        kernel,
        out_shape=jax.ShapeDtypeStruct((QROWS, HEADS * HD), jnp.bfloat16),
        in_specs=[far] * 5,
        out_specs=anywhere,
        scratch_shapes=[
            pltpu.SMEM(tile_lists.shape[::-1], jnp.int32), pltpu.SMEM(tile_counts.shape, jnp.int32), dma((2,)),
            held(2 * HALF), held(2 * HALF), held(HALF),
            held(PAIR), held(PAIR), held(ONE),
            held(PAIR), held(PAIR), held(ONE),
            held(5 * HALF),
            pltpu.VMEM((PAIR // TILE, TILE, HD), jnp.bfloat16),
            pltpu.VMEM((PAIR // TILE, VROWS, TILE), jnp.bfloat16),
            pltpu.VMEM((FT, 2 * HD, TILE), jnp.bfloat16),
            pltpu.VMEM((G * TILE, TILE), jnp.float32),
            pltpu.VMEM((G * TILE, TILE), jnp.float32),
            pltpu.VMEM((VROWS, TILE), jnp.float32),
            pltpu.VMEM((FT * GROUPS, G * TILE, TILE), jnp.float32),
            pltpu.VMEM((FT, 1, TILE), jnp.float32),
            dma((9,)), dma((10,)), dma((3,)), dma((12,)), dma((12,)), dma((2,)), dma((2,)), dma((3,)), dma,
        ],
        compiler_params=pltpu.CompilerParams(
            collective_id=0, has_side_effects=True, vmem_limit_bytes=52 * 1024 * 1024
        ),
        name="attention",
    )(tile_lists.T, tile_counts, queries, keys, values)


def solution(mesh):
    placed = (P(("blk", "uly"), None), P(("blk", "uly"), None), P(("blk", "uly"), None), P(), P())
    return jax.shard_map(
        per_device, mesh=mesh, in_specs=placed, out_specs=P(("blk", "uly"), None), check_vma=False
    )
```
